256 devices in a mesh: gx: 8 (over z), gy: 4 (over x), gz: 8 (over y, core).
Axes of the slice: x: 4, y: 4, z: 8, core: 2. Of those that a mesh axis runs over, the one named last changes fastest.
Arguments:
- port_rhs: float32 [4, 3, 32, 16, 2048], P(None, None, 'gx', 'gy', 'gz'), may hold values from -6 to 6
- edge_sign: int32 [3, 32, 16, 2048], P(None, 'gx', 'gy', 'gz'), may hold values from -1 to 1, as said below
- face_nu: float32 [3, 32, 16, 2048], P(None, 'gx', 'gy', 'gz'), may hold values from 0.05 to 1
- edge_sigma: float32 [3, 32, 16, 2048], P(None, 'gx', 'gy', 'gz'), may hold values from 0.1 to 2
- coarse_cols: int32 [4, 32, 16, 32], P(None, 'gx', 'gy', 'gz'), may hold values from 0 to 1023, as said below
- grad_interp: float32 [4, 32, 16, 2048], P(None, 'gx', 'gy', 'gz'), may hold values from 0.02 to 0.25
- vec_interp: float32 [4, 32, 16, 2048], P(None, 'gx', 'gy', 'gz'), may hold values from 0.02 to 0.25
- grad_coarse_inverse: float32 [1024, 1024], P(('gx', 'gy'))
- vec_coarse_inverse: float32 [3072, 3072], P(('gx', 'gy'))
Outputs:
- solution: float32 [4, 3, 32, 16, 2048], P(None, None, 'gx', 'gy', 'gz')
The draws below stay inside these ranges and needn't reach their ends.
Inputs may be any that keep to these rules, and one draw needn't show every extreme that they name: `edge_sign`: each entry is -1 or +1. `coarse_cols`: coarse node m belongs to the device of index m // 4 in the mesh's order (gx slowest, gz fastest); in every block the first entry names a node of the block's own device, the others nodes of its own device or of a device next to it along one axis.
All inputs are finite; a program needn't handle non-finite values.
Results may differ from the reference program's by a relative error of at most 0.000078.
Values sent between devices are 32-bit elements; how exact they have to be, the bound alone decides.
No kernel may reach another device: no remote copies, remote signals or barrier semaphores. Data moves between devices by JAX's collectives and lax.ppermute only.
A program may use at most 384 MiB of HBM per device.

```python
import math
import jax
import jax.numpy as jnp
from jax import lax

CX = 4
CY = 4
CZ = 256
PORTS = 4
COLS = 4
BLOCK = 64
CN_DEV = 4
NX = 32
NY = 16
NZ = 2048
NCN = 1024


def draw_edge_sign(key, part):
    key = jax.random.fold_in(key, 1)
    coins = jax.random.randint(key, (3, NX, NY, NZ), 0, 2)
    return (2 * coins - 1).astype(jnp.int32)


def draw_coarse_cols(key, part):
    key = jax.random.fold_in(key, 2)
    pick_key, node_key = jax.random.split(key)
    blocks_z = NZ // BLOCK
    per_device = CZ // BLOCK
    devices_x = NX // CX
    devices_y = NY // CY
    devices_z = NZ // CZ
    grid_shape = (COLS, NX, NY, blocks_z)
    owner_x = (jnp.arange(NX) // CX)[None, :, None, None]
    owner_y = (jnp.arange(NY) // CY)[None, None, :, None]
    owner_z = (jnp.arange(blocks_z) // per_device)[None, None, None, :]
    neighbour = jax.random.randint(pick_key, grid_shape, 0, 7)
    first_row = (jnp.arange(COLS) == 0)[:, None, None, None]
    neighbour = jnp.where(first_row, 0, neighbour)
    step_x = jnp.where(neighbour == 1, 1, 0) - jnp.where(neighbour == 2, 1, 0)
    step_y = jnp.where(neighbour == 3, 1, 0) - jnp.where(neighbour == 4, 1, 0)
    step_z = jnp.where(neighbour == 5, 1, 0) - jnp.where(neighbour == 6, 1, 0)
    near_x = jnp.clip(owner_x + step_x, 0, devices_x - 1)
    near_y = jnp.clip(owner_y + step_y, 0, devices_y - 1)
    near_z = jnp.clip(owner_z + step_z, 0, devices_z - 1)
    linear = (near_x * devices_y + near_y) * devices_z + near_z
    within = jax.random.randint(node_key, grid_shape, 0, CN_DEV)
    return (linear * CN_DEV + within).astype(jnp.int32)


def coarse_matrix(key, dimension):
    diag_key, off_key = jax.random.split(key)
    leading = jax.random.uniform(diag_key, (dimension,), jnp.float32, 0.5, 1.5)
    spread = jax.random.normal(off_key, (dimension, dimension), jnp.float32) * (0.5 / math.sqrt(dimension))
    rows = jnp.arange(dimension)[:, None]
    columns = jnp.arange(dimension)[None, :]
    return 0.02 * (jnp.where(rows == columns, leading[:, None], 0.0) + spread)


def draw_grad_coarse_inverse(key, part):
    key = jax.random.fold_in(key, 3)
    return coarse_matrix(key, NCN)


def draw_vec_coarse_inverse(key, part):
    key = jax.random.fold_in(key, 4)
    return coarse_matrix(key, 3 * NCN)


def steps_of(stream_key, dims, cuts, least, largest):
    factor_of, own = 1.0, jax.random.fold_in(stream_key, 6)
    for axis_at, shards_of in cuts:
        steps = jnp.exp(jax.random.uniform(jax.random.fold_in(own, axis_at), (shards_of,), jnp.float32, least / len(cuts), largest / len(cuts)))
        factor_of = factor_of * jnp.repeat(steps, dims[axis_at] // shards_of).reshape([-1 if axis == axis_at else 1 for axis in range(len(dims))])
    return factor_of


def centred(own_key, shape, width, bound, cuts=(), kind=jnp.bfloat16):
    values = width * jax.random.normal(own_key, shape, jnp.float32)
    if cuts:
        values = values * steps_of(own_key, shape, cuts, -0.22, 0.18)
    return jnp.clip(values, -bound, bound).astype(kind)


def setup_inputs(seed: int = 0) -> dict:
    splits = jax.random.split(jax.random.key(seed), 10)
    return {
        "port_rhs": centred(splits[0], (PORTS, 3, NX, NY, NZ), 1.0, 6.0, ((2, 8), (3, 4), (4, 8)), jnp.float32),
        "edge_sign": draw_edge_sign(jax.random.fold_in(splits[9], 71), 0),
        "face_nu": jnp.clip(jnp.exp(math.log(1.0) - 2.9957323 * jax.random.uniform(splits[2], (3, NX, NY, NZ), jnp.float32) ** steps_of(splits[2], (3, NX, NY, NZ), ((1, 8), (2, 4), (3, 8)), -0.2, 0.2)), 0.05, 1.0),
        "edge_sigma": jnp.clip(jnp.exp(math.log(2.0) - 2.9957323 * jax.random.uniform(splits[3], (3, NX, NY, NZ), jnp.float32) ** steps_of(splits[3], (3, NX, NY, NZ), ((1, 8), (2, 4), (3, 8)), -0.2, 0.2)), 0.1, 2.0),
        "coarse_cols": draw_coarse_cols(jax.random.fold_in(splits[9], 71), 0),
        "grad_interp": jnp.clip(0.02 + 0.23 * jax.random.uniform(splits[5], (COLS, NX, NY, NZ), jnp.float32) ** steps_of(splits[5], (COLS, NX, NY, NZ), ((1, 8), (2, 4), (3, 8)), -0.2, 0.2), 0.02, 0.25),
        "vec_interp": jnp.clip(0.02 + 0.23 * jax.random.uniform(splits[6], (COLS, NX, NY, NZ), jnp.float32) ** steps_of(splits[6], (COLS, NX, NY, NZ), ((1, 8), (2, 4), (3, 8)), -0.2, 0.2), 0.02, 0.25),
        "grad_coarse_inverse": draw_grad_coarse_inverse(jax.random.fold_in(splits[9], 71), 0),
        "vec_coarse_inverse": draw_vec_coarse_inverse(jax.random.fold_in(splits[9], 71), 0),
    }


def extract(values, start_x, start_y, start_z, extent):
    return values[..., start_x:start_x + extent[0], start_y:start_y + extent[1], start_z:start_z + extent[2]]


def shrink(values, margin):
    extent = tuple(length - 2 * margin for length in values.shape[-3:])
    return extract(values, margin, margin, margin, extent)


def offset(values, displacement):
    extent = tuple(length - 2 for length in values.shape[-3:])
    return extract(values, 1 + displacement[0], 1 + displacement[1], 1 + displacement[2], extent)


def unit_step(direction, amount):
    return tuple(amount if position == direction else 0 for position in range(3))


def row_norms(face_nu, edge_sigma):
    centre = (0, 0, 0)
    columns = []
    for direction in range(3):
        others = [candidate for candidate in range(3) if candidate != direction]
        summed = offset(edge_sigma[direction], centre)
        for normal in others:
            within = [candidate for candidate in others if candidate != normal][0]
            summed = summed + 4.0 * (offset(face_nu[normal], centre) + offset(face_nu[normal], unit_step(within, -1)))
        columns.append(summed)
    return jnp.stack(columns, 0)


def ahead_diff(values, direction, extent):
    beginning = unit_step(direction, 1)
    return extract(values, beginning[0], beginning[1], beginning[2], extent) - extract(values, 0, 0, 0, extent)


def behind_diff(values, direction, extent):
    beginning = unit_step(direction, -1)
    return extract(values, 1 + beginning[0], 1 + beginning[1], 1 + beginning[2], extent) - extract(values, 1, 1, 1, extent)


def operate(edge_field, orient, face_nu, edge_sigma):
    canonical = edge_field * orient
    outer_size = tuple(length - 1 for length in canonical.shape[-3:])
    inner_size = tuple(length - 2 for length in canonical.shape[-3:])
    part_zero = canonical[:, 0]
    part_one = canonical[:, 1]
    part_two = canonical[:, 2]
    curl_zero = ahead_diff(part_two, 1, outer_size) - ahead_diff(part_one, 2, outer_size)
    curl_one = ahead_diff(part_zero, 2, outer_size) - ahead_diff(part_two, 0, outer_size)
    curl_two = ahead_diff(part_one, 0, outer_size) - ahead_diff(part_zero, 1, outer_size)
    weights = extract(face_nu, 0, 0, 0, outer_size)
    flux_zero = weights[0] * curl_zero
    flux_one = weights[1] * curl_one
    flux_two = weights[2] * curl_two
    back_zero = behind_diff(flux_one, 2, inner_size) - behind_diff(flux_two, 1, inner_size)
    back_one = behind_diff(flux_two, 0, inner_size) - behind_diff(flux_zero, 2, inner_size)
    back_two = behind_diff(flux_zero, 1, inner_size) - behind_diff(flux_one, 0, inner_size)
    result = jnp.stack([back_zero, back_one, back_two], 1) + shrink(edge_sigma, 1) * shrink(canonical, 1)
    return result * shrink(orient, 1)


def restrict_nodes(residual, orient):
    canonical = residual * orient
    centre = (0, 0, 0)
    grad_part = None
    vec_parts = []
    for direction in range(3):
        at_node = offset(canonical[:, direction], centre)
        beneath = offset(canonical[:, direction], unit_step(direction, -1))
        if grad_part is None:
            grad_part = beneath - at_node
        else:
            grad_part = grad_part + beneath - at_node
        vec_parts.append(0.5 * (at_node + beneath))
    return grad_part, jnp.stack(vec_parts, 1)


def prolong_edges(nodal_field, orient):
    centre = (0, 0, 0)
    columns = []
    for direction in range(3):
        forward = unit_step(direction, 1)
        gradient = offset(nodal_field[:, 0], forward) - offset(nodal_field[:, 0], centre)
        average = 0.5 * (offset(nodal_field[:, 1 + direction], centre) + offset(nodal_field[:, 1 + direction], forward))
        columns.append(gradient + average)
    return jnp.stack(columns, 1) * orient


def coarse_terms(grad_part, vec_part, coarse_cols, grad_interp, vec_interp, coarse_count):
    block_shape = coarse_cols.shape + (BLOCK,)
    port_count = grad_part.shape[0]
    grad_weights = grad_interp.reshape(block_shape)
    vec_weights = vec_interp.reshape(block_shape)
    grad_blocks = jnp.einsum("rxyzb,kxyzb->rkxyz", grad_part.reshape((port_count,) + block_shape[1:]), grad_weights, precision=lax.Precision.HIGHEST)
    vec_blocks = jnp.einsum("rcxyzb,kxyzb->rckxyz", vec_part.reshape((port_count, 3) + block_shape[1:]), vec_weights, precision=lax.Precision.HIGHEST)
    flat_cols = coarse_cols.reshape(-1)
    coarse_grad = jnp.zeros((port_count, coarse_count), grad_blocks.dtype).at[:, flat_cols].add(grad_blocks.reshape(port_count, -1))
    coarse_vec = jnp.zeros((port_count, 3, coarse_count), vec_blocks.dtype).at[:, :, flat_cols].add(vec_blocks.reshape(port_count, 3, -1))
    return coarse_grad, coarse_vec.reshape(port_count, 3 * coarse_count)


def apply_rows(vector, rows):
    return lax.dot_general(vector, rows, (((1,), (1,)), ((), ())), precision=lax.Precision.HIGHEST)


def prolong_nodes(grad_values, vec_values, node_cols, grad_weights, vec_weights):
    port_count = grad_values.shape[0]
    coarse_count = grad_values.shape[1]
    grad_taken = jnp.take(grad_values, node_cols, axis=1)
    grad_node = jnp.sum(grad_taken * grad_weights, axis=1)
    vec_taken = jnp.take(vec_values.reshape(port_count, 3, coarse_count), node_cols, axis=2)
    vec_node = jnp.sum(vec_taken * vec_weights, axis=2)
    return jnp.concatenate([grad_node[:, None], vec_node], 1)


def smooth_first(rhs_wide, orient_wide, nu_wide, sigma_wide):
    orient_two = shrink(orient_wide, 1)
    diagonal = row_norms(nu_wide, sigma_wide) + (1.0 - orient_two * orient_two)
    rhs_two = shrink(rhs_wide, 1)
    direct = rhs_two / diagonal
    residual = shrink(rhs_two, 1) - operate(direct, orient_two, shrink(nu_wide, 1), shrink(sigma_wide, 1))
    grad_part, vec_part = restrict_nodes(residual, shrink(orient_wide, 2))
    return direct, residual, diagonal, grad_part, vec_part


def finish(direct, residual, diagonal, nodal_wide, orient_wide, nu_wide, sigma_wide):
    correction = prolong_edges(nodal_wide, shrink(orient_wide, 2))
    second = shrink(residual, 1) - operate(correction, shrink(orient_wide, 2), shrink(nu_wide, 2), shrink(sigma_wide, 2))
    return shrink(direct, 2) + shrink(correction, 1) + second / shrink(diagonal, 2)


def reference(port_rhs, edge_sign, face_nu, edge_sigma, coarse_cols, grad_interp, vec_interp, grad_coarse_inverse, vec_coarse_inverse):
    orient = edge_sign.astype(port_rhs.dtype)
    padding = ((0, 0), (3, 3), (3, 3), (3, 3))
    orient_wide = jnp.pad(orient, padding)
    nu_wide = jnp.pad(face_nu, padding)
    sigma_wide = jnp.pad(edge_sigma, padding)
    node_cols = jnp.broadcast_to(coarse_cols[..., None], coarse_cols.shape + (BLOCK,)).reshape(grad_interp.shape)
    coarse_count = grad_coarse_inverse.shape[0]

    def one_port(rhs_port):
        rhs_wide = jnp.pad(rhs_port[None], ((0, 0),) + padding)
        direct, residual, diagonal, grad_part, vec_part = smooth_first(rhs_wide, orient_wide, nu_wide, sigma_wide)
        coarse_grad, coarse_vec = coarse_terms(grad_part, vec_part, coarse_cols, grad_interp, vec_interp, coarse_count)
        grad_values = apply_rows(coarse_grad, grad_coarse_inverse)
        vec_values = apply_rows(coarse_vec, vec_coarse_inverse)
        nodal_field = prolong_nodes(grad_values, vec_values, node_cols, grad_interp, vec_interp)
        nodal_wide = jnp.pad(nodal_field, ((0, 0), (0, 0), (2, 2), (2, 2), (2, 2)))
        return finish(direct, residual, diagonal, nodal_wide, orient_wide, nu_wide, sigma_wide)[0]

    return lax.map(one_port, port_rhs)
```

```python
import jax
import jax.numpy as jnp
from jax import lax
from jax.experimental import pallas as pl
from jax.experimental.pallas import tpu as pltpu
from jax.sharding import PartitionSpec as P

F32 = jnp.float32
BF16 = jnp.bfloat16
HIGHEST = lax.Precision.HIGHEST
NT = (((1,), (1,)), ((), ()))
NN = (((1,), (0,)), ((), ()))

B, NU, SG, GI, VI, CP = 0, 12, 15, 18, 22, 26
PLANES = 27
HI = PLANES + 3
LO = PLANES + 9
GROUP = 32


def col_lane(zb, k):
    return 252 + k if zb == 3 else 4 * zb + k


def spec():
    return pl.BlockSpec(memory_space=pltpu.VMEM)


def call(body, outs, count, scratch=(), limit=24):
    return pl.pallas_call(
        body,
        out_shape=[jax.ShapeDtypeStruct(shape, dtype) for shape, dtype in outs],
        in_specs=[spec()] * count,
        out_specs=[spec()] * len(outs),
        scratch_shapes=list(scratch),
        compiler_params=pltpu.CompilerParams(vmem_limit_bytes=limit * 1024 * 1024),
    )


def own_plane(refs, plane, x):
    rhs, sign, nu, sigma, gi, vi, cp = refs
    if plane < NU:
        return rhs[plane // 3, plane % 3, x] * sign[plane % 3, x].astype(F32)
    if plane < SG:
        return nu[plane - NU, x]
    if plane < GI:
        return sigma[plane - SG, x]
    if plane < VI:
        return gi[plane - GI, x]
    if plane < CP:
        return vi[plane - VI, x]
    return cp[x]


def pack_y(rhs, sign, nu, sigma, gi, vi, cols, yhi, ylo, cp):
    lane = lax.broadcasted_iota(jnp.int32, (4, 256), 1)
    for x in range(4):
        plane = jnp.zeros((4, 256), F32)
        for k in range(4):
            for zb in range(4):
                plane = jnp.where(
                    lane == col_lane(zb, k), cols[k, x, :, zb : zb + 1].astype(F32), plane
                )
        cp[x] = plane
    refs = (rhs, sign, nu, sigma, gi, vi, cp)
    for plane in range(PLANES):
        for x in range(4):
            value = own_plane(refs, plane, x)
            yhi[plane, x : x + 1, :] = value[3:4]
            ylo[plane, x : x + 1, :] = value[0:1]
            if NU <= plane < SG:
                yhi[PLANES + plane - NU, x : x + 1, :] = value[2:3]
            if plane >= GI:
                ylo[PLANES + plane - GI, x : x + 1, :] = value[1:2]


def pack_x(rhs, sign, nu, sigma, gi, vi, cp, yhi, ylo, wide, xhi, xlo):
    refs = (rhs, sign, nu, sigma, gi, vi, cp)
    zero = jnp.zeros((1, 256), F32)
    for plane in range(PLANES):
        for x in range(4):
            far_minus = yhi[PLANES + plane - NU, x : x + 1, :] if NU <= plane < SG else zero
            far_plus = ylo[PLANES + plane - GI, x : x + 1, :] if plane >= GI else zero
            wide[plane, x, 0:1, :] = far_minus
            wide[plane, x, 1:2, :] = yhi[plane, x : x + 1, :]
            wide[plane, x, 2:6, :] = own_plane(refs, plane, x)
            wide[plane, x, 6:7, :] = ylo[plane, x : x + 1, :]
            wide[plane, x, 7:8, :] = far_plus
        xhi[plane] = wide[plane, 3]
        xlo[plane] = wide[plane, 0]
        if NU <= plane < SG:
            xhi[PLANES + plane - NU] = wide[plane, 2]
        if plane >= GI:
            xlo[PLANES + plane - GI] = wide[plane, 1]


def slab(refs, plane, x):
    wide, xhi, xlo = refs
    if x == 0:
        return xhi[PLANES + plane - NU] if NU <= plane < SG else None
    if x == 1:
        return xhi[plane]
    if x == 6:
        return xlo[plane]
    if x == 7:
        return xlo[PLANES + plane - GI] if plane >= GI else None
    return wide[plane, x - 2]


def pack_z(wide, xhi, xlo, zhi, zlo):
    refs = (wide, xhi, xlo)
    lane = lax.broadcasted_iota(jnp.int32, (8, 128), 1)
    for x in range(8):
        low = jnp.zeros((8, 128), F32)
        high = jnp.zeros((8, 128), F32)
        for plane in range(PLANES):
            value = slab(refs, plane, x)
            if value is None:
                continue
            here = lane // 4 == plane
            low = jnp.where(here, pltpu.roll(value[:, 0:128], 4 * plane, 1), low)
            high = jnp.where(here, pltpu.roll(value[:, 128:256], (4 * plane + 4) % 128, 1), high)
        zlo[x] = low
        zhi[x] = high


def ahead(values, axis):
    return pltpu.roll(values, values.shape[axis] - 1, axis)


def behind(values, axis):
    return pltpu.roll(values, 1, axis)


def operate(v0, v1, v2, nu0, nu1, nu2, sg0, sg1, sg2):
    a0, a1, a2 = v0[:5], v1[:5], v2[:5]
    f0 = nu0 * ((ahead(a2, 1) - a2) - (ahead(a1, 2) - a1))
    f1 = nu1 * ((ahead(a0, 2) - a0) - (v2[1:6] - a2))
    f2 = nu2 * ((v1[1:6] - a1) - (ahead(a0, 1) - a0))
    r0 = (behind(f1, 2) - f1) - (behind(f2, 1) - f2) + sg0 * a0
    r1 = (f2[0:4] - f2[1:5]) - (behind(f0, 2)[1:5] - f0[1:5]) + sg1 * v1[1:5]
    r2 = (behind(f0, 1)[1:5] - f0[1:5]) - (f1[0:4] - f1[1:5]) + sg2 * v2[1:5]
    return r0, r1, r2


def restrict(wide, xhi, xlo, zhi, zlo, coarse, keep, inverse, ext, base, linv, sums):
    refs = (wide, xhi, xlo)
    lane = lax.broadcasted_iota(jnp.int32, (8, 128), 1)
    zero = jnp.zeros((8, 256), F32)
    for plane in range(PLANES):
        target = base if plane < NU else ext
        at = plane if plane < NU else plane - NU
        for x in range(8):
            value = slab(refs, plane, x)
            target[at, x, :, 0:256] = zero if value is None else value
            plus = pltpu.roll(zlo[x], (128 - 4 * plane) % 128, 1)
            minus = pltpu.roll(zhi[x], (124 - 4 * plane) % 128, 1)
            target[at, x, :, 256:384] = jnp.where(
                lane < 4, plus, jnp.where(lane >= 124, minus, 0.0)
            )
    nu0, nu1, nu2 = ext[0], ext[1], ext[2]
    n0, n1, n2 = nu0[1:7], nu1[1:7], nu2[1:7]
    floor = 0.1
    linv[0] = 1.0 / jnp.maximum(
        ext[3, 1:7] + 4.0 * ((n2 + behind(n2, 1)) + (n1 + behind(n1, 2))), floor
    )
    linv[1] = 1.0 / jnp.maximum(
        ext[4, 1:7] + 4.0 * ((n2 + nu2[0:6]) + (n0 + behind(n0, 2))), floor
    )
    linv[2] = 1.0 / jnp.maximum(
        ext[5, 1:7] + 4.0 * ((n1 + nu1[0:6]) + (n0 + behind(n0, 1))), floor
    )
    for i in range(3):
        inverse[i] = linv[i, 1:5, 2:6, 0:256]
    pick = (
        lax.broadcasted_iota(jnp.int32, (8, 256), 1) // 64
        == lax.broadcasted_iota(jnp.int32, (8, 256), 0)
    ).astype(F32)

    def port(p, carry):
        b0, b1, b2 = base[3 * p], base[3 * p + 1], base[3 * p + 2]
        u0, u1, u2 = b0[1:7] * linv[0], b1[1:7] * linv[1], b2[1:7] * linv[2]
        r0, r1, r2 = operate(
            u0, u1, u2, ext[0, 1:6], ext[1, 1:6], ext[2, 1:6], ext[3, 1:6], ext[4, 2:6], ext[5, 2:6]
        )
        t0, t1, t2 = b0[1:6] - r0, b1[2:6] - r1, b2[2:6] - r2
        here = (t0[1:5], t1, t2)
        back = (t0[0:4], behind(t1, 1), behind(t2, 2))
        wide_u = (u0, u1, u2)
        parts = [((back[0] - here[0]) + (back[1] - here[1])) + (back[2] - here[2])]
        for i in range(3):
            kept = wide_u[i][1:5] + here[i] * linv[i, 1:5]
            keep[3 * p + i] = kept[:, 2:6, 0:256]
            parts.append(0.5 * (here[i] + back[i]))
        for kind in range(4):
            first = GI - NU if kind == 0 else VI - NU
            part = parts[kind][:, :, 0:256]
            products = [
                (part * ext[first + k, 2:6, :, 0:256]).reshape(32, 256) for k in range(4)
            ]
            sums[4 * kind + p] = lax.dot_general(
                pick,
                jnp.concatenate(products, 0),
                NT,
                precision=HIGHEST,
                preferred_element_type=F32,
            )
        return carry

    lax.fori_loop(0, 4, port, 0)

    mine = (lax.axis_index("gx"), lax.axis_index("gy"), lax.axis_index("gz"))
    row = lax.broadcasted_iota(jnp.int32, (8, 128), 0)
    rows = []
    for k in range(4):
        for x in range(4):
            plane = ext[CP - NU, x + 2]
            column = jnp.zeros((8, 128), F32)
            for zb in range(4):
                at = col_lane(zb, k)
                column = jnp.where(lane // 32 == zb, plane[:, at : at + 1], column)
            node = column.astype(jnp.int32)
            owner = node >> 2
            dx = (owner >> 5) - mine[0]
            dy = ((owner >> 3) & 3) - mine[1]
            dz = (owner & 7) - mine[2]
            side = jnp.where(dx == 1, 1, jnp.where(dx == -1, 2, 0))
            side = jnp.where(dy == 1, 3, jnp.where(dy == -1, 4, side))
            side = jnp.where(dz == 1, 5, jnp.where(dz == -1, 6, side))
            slot = 4 * side + (node & 3)
            own = (row >= 2) & (row < 6)
            rows.append(jnp.where(own & (slot == lane % 32), 1.0, 0.0))
    hot = jnp.concatenate(rows, 0)
    spread = lax.dot_general(
        sums[...].reshape(128, 128), hot, NN, precision=HIGHEST, preferred_element_type=F32
    ).reshape(16, 8, 128)
    block = lax.broadcasted_iota(jnp.int32, (16, 8, 128), 1)
    lanes = lax.broadcasted_iota(jnp.int32, (16, 8, 128), 2)
    total = jnp.sum(jnp.where(lanes // 32 == block, spread, 0.0), axis=1)
    total = total + pltpu.roll(total, 64, 1)
    total = total + pltpu.roll(total, 32, 1)
    quarter = lax.broadcasted_iota(jnp.int32, (4, 128), 1) // 32
    mixed = total[0:4]
    for kind in range(1, 4):
        mixed = jnp.where(quarter == kind, total[4 * kind : 4 * kind + 4], mixed)
    for g in range(GROUP):
        coarse[g] = mixed


def multiply(parts, grad_rows, vec_rows, out, stacked):
    for gx in range(8):
        for gy in range(4):
            for kind in range(4):
                stacked[16 * gx + 4 * kind : 16 * gx + 4 * kind + 4, 32 * gy : 32 * gy + 32] = parts[
                    4 * gx + gy, :, 32 * kind : 32 * kind + 32
                ]
    z = lax.axis_index("gz")
    row = lax.broadcasted_iota(jnp.int32, (128, 128), 0)
    lane = lax.broadcasted_iota(jnp.int32, (128, 128), 1)
    gy = row // 32
    side = (row % 32) >> 2
    gy_to = gy + jnp.where(side == 3, 1, 0) - jnp.where(side == 4, 1, 0)
    z_to = z + jnp.where(side == 5, 1, 0) - jnp.where(side == 6, 1, 0)
    hit = lane == 32 * gy_to + 4 * z_to + (row & 3)
    stay = jnp.where(hit & ((side == 0) | ((side >= 3) & (side <= 6))), 1.0, 0.0)
    forth = jnp.where(hit & (side == 1), 1.0, 0.0)
    back = jnp.where(hit & (side == 2), 1.0, 0.0)

    def spread(where):
        return lax.dot_general(
            stacked[...], where, NN, precision=HIGHEST, preferred_element_type=F32
        )

    stays, forths, backs = spread(stay), spread(forth), spread(back)
    tiles = []
    for gx in range(8):
        tile = stays[16 * gx : 16 * gx + 16]
        if gx > 0:
            tile = tile + forths[16 * gx - 16 : 16 * gx]
        if gx < 7:
            tile = tile + backs[16 * gx + 16 : 16 * gx + 32]
        tiles.append(tile)
    vector = jnp.concatenate(tiles, 1)
    grad = lax.dot_general(
        vector[0:8], grad_rows[...], NT, precision=HIGHEST, preferred_element_type=F32
    )[0:4]
    vec = jnp.zeros((4, 96), F32)
    for i in range(3):
        start = 4 + 4 * i
        half = 8 * (start // 8)
        product = lax.dot_general(
            vector[half : half + 8],
            vec_rows[:, 1024 * i : 1024 * i + 1024],
            NT,
            precision=HIGHEST,
            preferred_element_type=F32,
        )
        vec = vec + product[start - half : start - half + 4]
    for z_at in range(8):
        out[z_at, :, 0:32] = grad
        out[z_at, :, 32:128] = vec


def finish(values, ext, keep, inverse, sign, out, dense, nodal):
    for g in range(GROUP):
        dense[0:4, 32 * g : 32 * g + 32] = values[g, :, 0:32]
        for c in range(3):
            q = 3 * g + c
            row = 4 + 4 * (q // 32)
            at = 32 * (q % 32)
            dense[row : row + 4, at : at + 32] = values[g, :, 32 + 32 * c : 64 + 32 * c]
    whole = dense[...]
    top = whole.astype(BF16)
    rest = whole - top.astype(F32)
    middle = rest.astype(BF16)
    bottom = (rest - middle.astype(F32)).astype(BF16)
    split = jnp.concatenate([top, middle, bottom], 0)
    blank = jnp.zeros((48, 1024), BF16)
    sides = (jnp.concatenate([split, blank], 0), jnp.concatenate([blank, split], 0))
    select_row = lax.broadcasted_iota(jnp.int32, (96, 2048), 0)
    select_lane = lax.broadcasted_iota(jnp.int32, (96, 2048), 1)
    select = jnp.where(
        ((select_row % 16) == (select_lane // 128))
        & ((select_row // 48) == ((select_lane // 64) % 2)),
        1.0,
        0.0,
    ).astype(BF16)
    node = lax.broadcasted_iota(jnp.int32, (8, 1024), 1)
    lanes = (
        [col_lane(0, k) for k in range(4)],
        [col_lane(1, k) for k in range(4)],
        [col_lane(2, k) for k in range(4)],
        [col_lane(3, k) for k in range(4)],
        [256 + k for k in range(4)],
        [380 + k for k in range(4)],
    )
    for tile in range(3):
        taken = jnp.zeros((256, 96), F32)
        for half in range(2):
            rows = []
            for k in range(4):
                at = lanes[2 * tile + half][k]
                for x in range(8):
                    column = ext[CP - NU, x, :, at : at + 1].astype(jnp.int32)
                    rows.append(jnp.where(column == node, 1.0, 0.0).astype(F32))
            hot = jnp.concatenate(rows, 0).astype(BF16)
            taken = taken + lax.dot_general(hot, sides[half], NT, preferred_element_type=F32)
        taken = taken.astype(BF16)
        for kind in range(4):
            first = GI - NU if kind == 0 else VI - NU
            spread = lax.dot_general(
                taken,
                select[:, 512 * kind : 512 * kind + 512],
                NN,
                preferred_element_type=F32,
            )
            for p in range(4):
                total = jnp.zeros((8, 8, 128), F32)
                for k in range(4):
                    total = total + ext[first + k, :, :, 128 * tile : 128 * tile + 128] * spread[
                        64 * k : 64 * k + 64, 128 * p : 128 * p + 128
                    ].reshape(8, 8, 128)
                nodal[4 * kind + p, :, :, 128 * tile : 128 * tile + 128] = total

    shape = (6, 8, 384)
    x_at = lax.broadcasted_iota(jnp.int32, shape, 0)
    y_at = lax.broadcasted_iota(jnp.int32, shape, 1)
    z_at = lax.broadcasted_iota(jnp.int32, shape, 2)
    outside_x = (x_at == 0) & (lax.axis_index("gx") == 0)
    outside_y = (y_at == 1) & (lax.axis_index("gy") == 0)
    outside_z = (z_at == 383) & (lax.axis_index("gz") == 0)

    def port(p, carry):
        g = nodal[p]
        v0, v1, v2 = nodal[4 + p], nodal[8 + p], nodal[12 + p]
        here = g[1:7]
        c0 = (g[2:8] - here) + 0.5 * (v0[1:7] + v0[2:8])
        c1 = (ahead(here, 1) - here) + 0.5 * (v1[1:7] + ahead(v1[1:7], 1))
        c2 = (ahead(here, 2) - here) + 0.5 * (v2[1:7] + ahead(v2[1:7], 2))
        c0 = jnp.where(outside_x, 0.0, c0)
        c1 = jnp.where(outside_y, 0.0, c1)
        c2 = jnp.where(outside_z, 0.0, c2)
        r0, r1, r2 = operate(
            c0, c1, c2, ext[0, 1:6], ext[1, 1:6], ext[2, 1:6], ext[3, 1:6], ext[4, 2:6], ext[5, 2:6]
        )
        fields = ((c0[1:5], r0[1:5]), (c1[1:5], r1), (c2[1:5], r2))
        for i in range(3):
            c, r = fields[i]
            w = keep[3 * p + i] + (c[:, 2:6, 0:256] - r[:, 2:6, 0:256] * inverse[i])
            out[p, i] = sign[i].astype(F32) * w
        return carry

    lax.fori_loop(0, 4, port, 0)


def exchange(to_plus, to_minus, axis):
    count = lax.axis_size(axis)
    up = [(i, i + 1) for i in range(count - 1)]
    down = [(i + 1, i) for i in range(count - 1)]
    return lax.ppermute(to_plus, axis, up), lax.ppermute(to_minus, axis, down)


def per_device(rhs, sign, nu, sigma, cols, gi, vi, grad_rows, vec_rows):
    yhi, ylo, cp = call(
        pack_y,
        [((HI, 4, 256), F32), ((LO, 4, 256), F32), ((4, 4, 256), F32)],
        7,
    )(rhs, sign, nu, sigma, gi, vi, cols)
    yhi, ylo = exchange(yhi, ylo, "gy")
    wide, xhi, xlo = call(
        pack_x,
        [((PLANES, 4, 8, 256), F32), ((HI, 8, 256), F32), ((LO, 8, 256), F32)],
        9,
    )(rhs, sign, nu, sigma, gi, vi, cp, yhi, ylo)
    xhi, xlo = exchange(xhi, xlo, "gx")
    zhi, zlo = call(pack_z, [((8, 8, 128), F32)] * 2, 3)(wide, xhi, xlo)
    zhi, zlo = exchange(zhi, zlo, "gz")
    coarse, keep, inverse, ext = call(
        restrict,
        [
            ((GROUP, 4, 128), F32),
            ((12, 4, 4, 256), F32),
            ((3, 4, 4, 256), F32),
            ((PLANES - NU, 8, 8, 384), F32),
        ],
        5,
        [
            pltpu.VMEM((NU, 8, 8, 384), F32),
            pltpu.VMEM((3, 6, 8, 384), F32),
            pltpu.VMEM((16, 8, 128), F32),
        ],
    )(wide, xhi, xlo, zhi, zlo)
    coarse = lax.all_to_all(coarse, ("gx", "gy"), 0, 0)
    (partial,) = call(
        multiply, [((8, 4, 128), F32)], 3, [pltpu.VMEM((128, 128), F32)]
    )(coarse, grad_rows, vec_rows)
    partial = lax.all_to_all(partial, "gz", 0, 0)
    values = jnp.broadcast_to(jnp.sum(partial, 0)[None], (GROUP, 4, 128))
    values = lax.all_to_all(values, ("gx", "gy"), 0, 0)
    (out,) = call(
        finish,
        [((4, 3, 4, 4, 256), F32)],
        5,
        [pltpu.VMEM((16, 1024), F32), pltpu.VMEM((16, 8, 8, 384), F32)],
    )(values, ext, keep, inverse, sign)
    return out


def solution(mesh):
    grid = P(None, "gx", "gy", "gz")
    return jax.shard_map(
        per_device,
        mesh=mesh,
        in_specs=(
            P(None, None, "gx", "gy", "gz"),
            grid,
            grid,
            grid,
            grid,
            grid,
            grid,
            P(("gx", "gy"), None),
            P(("gx", "gy"), None),
        ),
        out_specs=P(None, None, "gx", "gy", "gz"),
        check_vma=False,
    )
```

```python
import jax
import jax.numpy as jnp
from jax import lax
from jax.experimental import pallas as pl
from jax.experimental.pallas import tpu as pltpu
from jax.sharding import PartitionSpec as P

F32 = jnp.float32
BF16 = jnp.bfloat16
HIGHEST = lax.Precision.HIGHEST
NT = (((1,), (1,)), ((), ()))
NN = (((1,), (0,)), ((), ()))

B, NU, SG, GI, VI, CP = 0, 12, 15, 18, 22, 26
PLANES = 27
GROUP = 32


def faces(axis):
    hi = [(plane, 0) for plane in range(PLANES)]
    hi += [(NU + i, 1) for i in range(3) if i != axis]
    lo = [(plane, 0) for plane in range(PLANES) if plane >= NU or plane % 3 != axis]
    lo = [(plane, layer) for plane, layer in lo if plane != SG + axis]
    return hi, lo


def depth(axis):
    return max(len(face) for face in faces(axis))


def col_lane(zb, k):
    return 252 + k if zb == 3 else 4 * zb + k


def call(body, outs, specs, scratch=(), limit=24):
    return pl.pallas_call(
        body,
        out_shape=[jax.ShapeDtypeStruct(shape, dtype) for shape, dtype in outs],
        in_specs=[pl.BlockSpec(memory_space=space) for space in specs],
        out_specs=[pl.BlockSpec(memory_space=pltpu.VMEM)] * len(outs),
        scratch_shapes=list(scratch),
        compiler_params=pltpu.CompilerParams(vmem_limit_bytes=limit * 1024 * 1024),
    )


def is_even(axis):
    return lax.rem(lax.axis_index(axis), 2) == 0


def send(even, hi, lo, first, second):
    @pl.when(even)
    def _():
        hi(first)
        lo(second)

    @pl.when(jnp.logical_not(even))
    def _():
        hi(second)
        lo(first)


def pack_y(rhs, sign, nu, sigma, gi, vi, cols, own, first, second, rhs_v, sign_v, cols_v, sems):
    copies = [
        pltpu.make_async_copy(rhs, rhs_v, sems.at[0]),
        pltpu.make_async_copy(sign, sign_v, sems.at[1]),
        pltpu.make_async_copy(cols, cols_v, sems.at[2]),
        pltpu.make_async_copy(nu, own.at[NU:SG], sems.at[3]),
        pltpu.make_async_copy(sigma, own.at[SG:GI], sems.at[4]),
        pltpu.make_async_copy(gi, own.at[GI:VI], sems.at[5]),
        pltpu.make_async_copy(vi, own.at[VI:CP], sems.at[6]),
    ]
    for copy in copies:
        copy.start()
    for copy in copies:
        copy.wait()
    lane = lax.broadcasted_iota(jnp.int32, (4, 256), 1)
    for x in range(4):
        plane = jnp.zeros((4, 256), F32)
        for k in range(4):
            for zb in range(4):
                plane = jnp.where(
                    lane == col_lane(zb, k), cols_v[k, x, :, zb : zb + 1].astype(F32), plane
                )
        own[CP, x] = plane
    for i in range(3):
        sign_of = sign_v[i].astype(F32)
        for p in range(4):
            own[3 * p + i] = rhs_v[p, i] * sign_of
    hi_list, lo_list = faces(1)

    def hi(target):
        for at, (plane, layer) in enumerate(hi_list):
            for x in range(4):
                target[at, x : x + 1, :] = own[plane, x, 3 - layer : 4 - layer, :]

    def lo(target):
        for at, (plane, layer) in enumerate(lo_list):
            for x in range(4):
                target[at, x : x + 1, :] = own[plane, x, layer : layer + 1, :]

    send(is_even("gy"), hi, lo, first, second)


def pack_x(own, y_first, y_second, wide, first, second):
    hi_list, lo_list = faces(1)
    hi_at = {entry: at for at, entry in enumerate(hi_list)}
    lo_at = {entry: at for at, entry in enumerate(lo_list)}

    def fill(minus, plus):
        zero = jnp.zeros((1, 256), F32)
        for plane in range(PLANES):
            for x in range(4):
                for row, where, source, key in (
                    (0, hi_at, minus, (plane, 1)),
                    (1, hi_at, minus, (plane, 0)),
                    (6, lo_at, plus, (plane, 0)),
                    (7, lo_at, plus, (plane, 1)),
                ):
                    value = source[where[key], x : x + 1, :] if key in where else zero
                    wide[plane, x, row : row + 1, :] = value
                wide[plane, x, 2:6, :] = own[plane, x]

    even_y = is_even("gy")

    @pl.when(even_y)
    def _():
        fill(y_second, y_first)

    @pl.when(jnp.logical_not(even_y))
    def _():
        fill(y_first, y_second)

    hi_x, lo_x = faces(0)

    def hi(target):
        for at, (plane, layer) in enumerate(hi_x):
            target[at] = wide[plane, 3 - layer]

    def lo(target):
        for at, (plane, layer) in enumerate(lo_x):
            target[at] = wide[plane, layer]

    send(is_even("gx"), hi, lo, first, second)


def slab_source(plane, x):
    hi_x, lo_x = faces(0)
    if 2 <= x < 6:
        return "own", x - 2
    side, entries, layer = ("minus", hi_x, 1 - x) if x < 2 else ("plus", lo_x, x - 6)
    key = (plane, layer)
    return (side, entries.index(key)) if key in entries else (None, None)


def pack_z(wide, x_first, x_second, first, second):
    lane = lax.broadcasted_iota(jnp.int32, (8, 128), 1)

    def fill(minus, plus, hi, lo):
        for x in range(8):
            low = jnp.zeros((8, 128), F32)
            high = jnp.zeros((8, 128), F32)
            for plane in range(PLANES):
                side, at = slab_source(plane, x)
                if side is None:
                    continue
                source = wide.at[plane, at] if side == "own" else (minus if side == "minus" else plus).at[at]
                here = lane // 4 == plane
                low = jnp.where(here, pltpu.roll(source[:, 0:128], 4 * plane, 1), low)
                high = jnp.where(
                    here, pltpu.roll(source[:, 128:256], (4 * plane + 4) % 128, 1), high
                )
            lo[x] = low
            hi[x] = high

    even_x, even_z = is_even("gx"), is_even("gz")
    for x_even in (True, False):
        for z_even in (True, False):

            @pl.when((even_x == x_even) & (even_z == z_even))
            def _(x_even=x_even, z_even=z_even):
                minus, plus = (x_second, x_first) if x_even else (x_first, x_second)
                hi, lo = (first, second) if z_even else (second, first)
                fill(minus, plus, hi, lo)


def ahead(values, axis):
    return pltpu.roll(values, values.shape[axis] - 1, axis)


def behind(values, axis):
    return pltpu.roll(values, 1, axis)


def operate(v0, v1, v2, nu0, nu1, nu2, sg0, sg1, sg2):
    a0, a1, a2 = v0[:5], v1[:5], v2[:5]
    f0 = nu0 * ((ahead(a2, 1) - a2) - (ahead(a1, 2) - a1))
    f1 = nu1 * ((ahead(a0, 2) - a0) - (v2[1:6] - a2))
    f2 = nu2 * ((v1[1:6] - a1) - (ahead(a0, 1) - a0))
    r0 = (behind(f1, 2) - f1) - (behind(f2, 1) - f2) + sg0 * a0
    r1 = (f2[0:4] - f2[1:5]) - (behind(f0, 2)[1:5] - f0[1:5]) + sg1 * v1[1:5]
    r2 = (behind(f0, 1)[1:5] - f0[1:5]) - (f1[0:4] - f1[1:5]) + sg2 * v2[1:5]
    return r0, r1, r2


def restrict(
    wide, x_first, x_second, z_first, z_second, coarse, keep, inverse, ext, base, linv, sums
):
    lane = lax.broadcasted_iota(jnp.int32, (8, 128), 1)
    even_x, even_z = is_even("gx"), is_even("gz")

    def place(plane):
        return (base, plane) if plane < NU else (ext, plane - NU)

    def fill(minus, plus):
        zero = jnp.zeros((8, 256), F32)
        for plane in range(PLANES):
            target, to = place(plane)
            for x in (0, 1, 6, 7):
                side, at = slab_source(plane, x)
                value = zero if side is None else (minus if side == "minus" else plus)[at]
                target[to, x, :, 0:256] = value

    @pl.when(even_x)
    def _():
        fill(x_second, x_first)

    @pl.when(jnp.logical_not(even_x))
    def _():
        fill(x_first, x_second)

    base[:, 2:6, :, 0:256] = wide[0:NU]
    ext[:, 2:6, :, 0:256] = wide[NU:PLANES]
    for x in range(8):
        before = jnp.where(even_z, z_second[x], z_first[x])
        after = jnp.where(even_z, z_first[x], z_second[x])
        for plane in range(PLANES):
            target, to = place(plane)
            target[to, x, :, 256:384] = jnp.where(
                lane < 4,
                pltpu.roll(after, (128 - 4 * plane) % 128, 1),
                jnp.where(lane >= 124, pltpu.roll(before, (124 - 4 * plane) % 128, 1), 0.0),
            )
    nu0, nu1, nu2 = ext[0], ext[1], ext[2]
    n0, n1, n2 = nu0[1:7], nu1[1:7], nu2[1:7]
    floor = 0.1
    linv[0] = 1.0 / jnp.maximum(
        ext[3, 1:7] + 4.0 * ((n2 + behind(n2, 1)) + (n1 + behind(n1, 2))), floor
    )
    linv[1] = 1.0 / jnp.maximum(
        ext[4, 1:7] + 4.0 * ((n2 + nu2[0:6]) + (n0 + behind(n0, 2))), floor
    )
    linv[2] = 1.0 / jnp.maximum(
        ext[5, 1:7] + 4.0 * ((n1 + nu1[0:6]) + (n0 + behind(n0, 1))), floor
    )
    for i in range(3):
        inverse[i] = linv[i, 1:5, 2:6, 0:256]
    pick = (
        lax.broadcasted_iota(jnp.int32, (8, 256), 1) // 64
        == lax.broadcasted_iota(jnp.int32, (8, 256), 0)
    ).astype(F32)

    def port(p, carry):
        b0, b1, b2 = base[3 * p], base[3 * p + 1], base[3 * p + 2]
        u0, u1, u2 = b0[1:7] * linv[0], b1[1:7] * linv[1], b2[1:7] * linv[2]
        r0, r1, r2 = operate(
            u0, u1, u2, ext[0, 1:6], ext[1, 1:6], ext[2, 1:6], ext[3, 1:6], ext[4, 2:6], ext[5, 2:6]
        )
        t0, t1, t2 = b0[1:6] - r0, b1[2:6] - r1, b2[2:6] - r2
        here = (t0[1:5], t1, t2)
        back = (t0[0:4], behind(t1, 1), behind(t2, 2))
        wide_u = (u0, u1, u2)
        parts = [((back[0] - here[0]) + (back[1] - here[1])) + (back[2] - here[2])]
        for i in range(3):
            kept = wide_u[i][1:5] + here[i] * linv[i, 1:5]
            keep[3 * p + i] = kept[:, 2:6, 0:256]
            parts.append(0.5 * (here[i] + back[i]))
        for kind in range(4):
            first = GI - NU if kind == 0 else VI - NU
            part = parts[kind][:, :, 0:256]
            products = [
                (part * ext[first + k, 2:6, :, 0:256]).reshape(32, 256) for k in range(4)
            ]
            sums[4 * kind + p] = lax.dot_general(
                pick,
                jnp.concatenate(products, 0),
                NT,
                precision=HIGHEST,
                preferred_element_type=F32,
            )
        return carry

    lax.fori_loop(0, 4, port, 0)

    mine = (lax.axis_index("gx"), lax.axis_index("gy"), lax.axis_index("gz"))
    row = lax.broadcasted_iota(jnp.int32, (8, 128), 0)
    rows = []
    for k in range(4):
        for x in range(4):
            plane = ext[CP - NU, x + 2]
            column = jnp.zeros((8, 128), F32)
            for zb in range(4):
                at = col_lane(zb, k)
                column = jnp.where(lane // 32 == zb, plane[:, at : at + 1], column)
            node = column.astype(jnp.int32)
            owner = node >> 2
            dx = (owner >> 5) - mine[0]
            dy = ((owner >> 3) & 3) - mine[1]
            dz = (owner & 7) - mine[2]
            side = jnp.where(dx == 1, 1, jnp.where(dx == -1, 2, 0))
            side = jnp.where(dy == 1, 3, jnp.where(dy == -1, 4, side))
            side = jnp.where(dz == 1, 5, jnp.where(dz == -1, 6, side))
            slot = 4 * side + (node & 3)
            own = (row >= 2) & (row < 6)
            rows.append(jnp.where(own & (slot == lane % 32), 1.0, 0.0))
    hot = jnp.concatenate(rows, 0)
    spread = lax.dot_general(
        sums[...].reshape(128, 128), hot, NN, precision=HIGHEST, preferred_element_type=F32
    ).reshape(16, 8, 128)
    block = lax.broadcasted_iota(jnp.int32, (16, 8, 128), 1)
    lanes = lax.broadcasted_iota(jnp.int32, (16, 8, 128), 2)
    total = jnp.sum(jnp.where(lanes // 32 == block, spread, 0.0), axis=1)
    total = total + pltpu.roll(total, 64, 1)
    total = total + pltpu.roll(total, 32, 1)
    quarter = lax.broadcasted_iota(jnp.int32, (4, 128), 1) // 32
    mixed = total[0:4]
    for kind in range(1, 4):
        mixed = jnp.where(quarter == kind, total[4 * kind : 4 * kind + 4], mixed)
    for g in range(GROUP):
        coarse[g] = mixed


def multiply(parts, grad_rows, vec_rows, out, stacked):
    for gx in range(8):
        for gy in range(4):
            for kind in range(4):
                stacked[16 * gx + 4 * kind : 16 * gx + 4 * kind + 4, 32 * gy : 32 * gy + 32] = parts[
                    4 * gx + gy, :, 32 * kind : 32 * kind + 32
                ]
    z = lax.axis_index("gz")
    row = lax.broadcasted_iota(jnp.int32, (128, 128), 0)
    lane = lax.broadcasted_iota(jnp.int32, (128, 128), 1)
    gy = row // 32
    side = (row % 32) >> 2
    gy_to = gy + jnp.where(side == 3, 1, 0) - jnp.where(side == 4, 1, 0)
    z_to = z + jnp.where(side == 5, 1, 0) - jnp.where(side == 6, 1, 0)
    hit = lane == 32 * gy_to + 4 * z_to + (row & 3)
    stay = jnp.where(hit & ((side == 0) | ((side >= 3) & (side <= 6))), 1.0, 0.0)
    forth = jnp.where(hit & (side == 1), 1.0, 0.0)
    back = jnp.where(hit & (side == 2), 1.0, 0.0)

    def spread(where):
        return lax.dot_general(
            stacked[...], where, NN, precision=HIGHEST, preferred_element_type=F32
        )

    stays, forths, backs = spread(stay), spread(forth), spread(back)
    tiles = []
    for gx in range(8):
        tile = stays[16 * gx : 16 * gx + 16]
        if gx > 0:
            tile = tile + forths[16 * gx - 16 : 16 * gx]
        if gx < 7:
            tile = tile + backs[16 * gx + 16 : 16 * gx + 32]
        tiles.append(tile)
    vector = jnp.concatenate(tiles, 1)
    grad = lax.dot_general(
        vector[0:8], grad_rows[...], NT, precision=HIGHEST, preferred_element_type=F32
    )[0:4]
    vec = jnp.zeros((4, 96), F32)
    for i in range(3):
        start = 4 + 4 * i
        half = 8 * (start // 8)
        product = lax.dot_general(
            vector[half : half + 8],
            vec_rows[:, 1024 * i : 1024 * i + 1024],
            NT,
            precision=HIGHEST,
            preferred_element_type=F32,
        )
        vec = vec + product[start - half : start - half + 4]
    for z_at in range(8):
        out[z_at, :, 0:32] = grad
        out[z_at, :, 32:128] = vec


def finish(values, ext, keep, inverse, sign, out, dense, nodal):
    for g in range(GROUP):
        dense[0:4, 32 * g : 32 * g + 32] = values[g, :, 0:32]
        for c in range(3):
            q = 3 * g + c
            row = 4 + 4 * (q // 32)
            at = 32 * (q % 32)
            dense[row : row + 4, at : at + 32] = values[g, :, 32 + 32 * c : 64 + 32 * c]
    whole = dense[...]
    top = whole.astype(BF16)
    rest = whole - top.astype(F32)
    middle = rest.astype(BF16)
    bottom = (rest - middle.astype(F32)).astype(BF16)
    split = jnp.concatenate([top, middle, bottom], 0)
    blank = jnp.zeros((48, 1024), BF16)
    sides = (jnp.concatenate([split, blank], 0), jnp.concatenate([blank, split], 0))
    select_row = lax.broadcasted_iota(jnp.int32, (96, 2048), 0)
    select_lane = lax.broadcasted_iota(jnp.int32, (96, 2048), 1)
    select = jnp.where(
        ((select_row % 16) == (select_lane // 128))
        & ((select_row // 48) == ((select_lane // 64) % 2)),
        1.0,
        0.0,
    ).astype(BF16)
    node = lax.broadcasted_iota(jnp.int32, (8, 1024), 1)
    lanes = (
        [col_lane(0, k) for k in range(4)],
        [col_lane(1, k) for k in range(4)],
        [col_lane(2, k) for k in range(4)],
        [col_lane(3, k) for k in range(4)],
        [256 + k for k in range(4)],
        [380 + k for k in range(4)],
    )
    for tile in range(3):
        taken = jnp.zeros((256, 96), F32)
        for half in range(2):
            rows = []
            for k in range(4):
                at = lanes[2 * tile + half][k]
                for x in range(8):
                    column = ext[CP - NU, x, :, at : at + 1].astype(jnp.int32)
                    rows.append(jnp.where(column == node, 1.0, 0.0).astype(F32))
            hot = jnp.concatenate(rows, 0).astype(BF16)
            taken = taken + lax.dot_general(hot, sides[half], NT, preferred_element_type=F32)
        taken = taken.astype(BF16)
        for kind in range(4):
            first = GI - NU if kind == 0 else VI - NU
            spread = lax.dot_general(
                taken,
                select[:, 512 * kind : 512 * kind + 512],
                NN,
                preferred_element_type=F32,
            )
            for p in range(4):
                total = jnp.zeros((8, 8, 128), F32)
                for k in range(4):
                    total = total + ext[first + k, :, :, 128 * tile : 128 * tile + 128] * spread[
                        64 * k : 64 * k + 64, 128 * p : 128 * p + 128
                    ].reshape(8, 8, 128)
                nodal[4 * kind + p, :, :, 128 * tile : 128 * tile + 128] = total

    shape = (6, 8, 384)
    x_at = lax.broadcasted_iota(jnp.int32, shape, 0)
    y_at = lax.broadcasted_iota(jnp.int32, shape, 1)
    z_at = lax.broadcasted_iota(jnp.int32, shape, 2)
    outside_x = (x_at == 0) & (lax.axis_index("gx") == 0)
    outside_y = (y_at == 1) & (lax.axis_index("gy") == 0)
    outside_z = (z_at == 383) & (lax.axis_index("gz") == 0)

    def port(p, carry):
        g = nodal[p]
        v0, v1, v2 = nodal[4 + p], nodal[8 + p], nodal[12 + p]
        here = g[1:7]
        c0 = (g[2:8] - here) + 0.5 * (v0[1:7] + v0[2:8])
        c1 = (ahead(here, 1) - here) + 0.5 * (v1[1:7] + ahead(v1[1:7], 1))
        c2 = (ahead(here, 2) - here) + 0.5 * (v2[1:7] + ahead(v2[1:7], 2))
        c0 = jnp.where(outside_x, 0.0, c0)
        c1 = jnp.where(outside_y, 0.0, c1)
        c2 = jnp.where(outside_z, 0.0, c2)
        r0, r1, r2 = operate(
            c0, c1, c2, ext[0, 1:6], ext[1, 1:6], ext[2, 1:6], ext[3, 1:6], ext[4, 2:6], ext[5, 2:6]
        )
        fields = ((c0[1:5], r0[1:5]), (c1[1:5], r1), (c2[1:5], r2))
        for i in range(3):
            c, r = fields[i]
            w = keep[3 * p + i] + (c[:, 2:6, 0:256] - r[:, 2:6, 0:256] * inverse[i])
            out[p, i] = sign[i].astype(F32) * w
        return carry

    lax.fori_loop(0, 4, port, 0)


def exchange(first, second, axis):
    count = lax.axis_size(axis)

    def pairs(start):
        found = []
        for i in range(start, count - 1, 2):
            found += [(i, i + 1), (i + 1, i)]
        return found

    return lax.ppermute(first, axis, pairs(0)), lax.ppermute(second, axis, pairs(1))


def per_device(rhs, sign, nu, sigma, cols, gi, vi, grad_rows, vec_rows):
    vmem = pltpu.VMEM
    own, first, second = call(
        pack_y,
        [((PLANES, 4, 4, 256), F32)] + [((depth(1), 4, 256), F32)] * 2,
        [pltpu.HBM] * 7,
        [
            pltpu.VMEM((4, 3, 4, 4, 256), F32),
            pltpu.VMEM((3, 4, 4, 256), jnp.int32),
            pltpu.VMEM((4, 4, 4, 4), jnp.int32),
            pltpu.SemaphoreType.DMA((7,)),
        ],
    )(rhs, sign, nu, sigma, gi, vi, cols)
    first, second = exchange(first, second, "gy")
    wide, x_first, x_second = call(
        pack_x,
        [((PLANES, 4, 8, 256), F32)] + [((depth(0), 8, 256), F32)] * 2,
        [vmem] * 3,
    )(own, first, second)
    x_first, x_second = exchange(x_first, x_second, "gx")
    z_first, z_second = call(pack_z, [((8, 8, 128), F32)] * 2, [vmem] * 3)(
        wide, x_first, x_second
    )
    z_first, z_second = exchange(z_first, z_second, "gz")
    coarse, keep, inverse, ext = call(
        restrict,
        [
            ((GROUP, 4, 128), F32),
            ((12, 4, 4, 256), F32),
            ((3, 4, 4, 256), F32),
            ((PLANES - NU, 8, 8, 384), F32),
        ],
        [vmem] * 5,
        [
            pltpu.VMEM((NU, 8, 8, 384), F32),
            pltpu.VMEM((3, 6, 8, 384), F32),
            pltpu.VMEM((16, 8, 128), F32),
        ],
    )(wide, x_first, x_second, z_first, z_second)
    coarse = lax.all_to_all(coarse, ("gx", "gy"), 0, 0)
    (partial,) = call(
        multiply, [((8, 4, 128), F32)], [vmem] * 3, [pltpu.VMEM((128, 128), F32)]
    )(coarse, grad_rows, vec_rows)
    partial = lax.all_to_all(partial, "gz", 0, 0)
    values = jnp.broadcast_to(jnp.sum(partial, 0)[None], (GROUP, 4, 128))
    values = lax.all_to_all(values, ("gx", "gy"), 0, 0)
    (out,) = call(
        finish,
        [((4, 3, 4, 4, 256), F32)],
        [vmem] * 5,
        [pltpu.VMEM((16, 1024), F32), pltpu.VMEM((16, 8, 8, 384), F32)],
    )(values, ext, keep, inverse, sign)
    return out


def solution(mesh):
    grid = P(None, "gx", "gy", "gz")
    return jax.shard_map(
        per_device,
        mesh=mesh,
        in_specs=(
            P(None, None, "gx", "gy", "gz"),
            grid,
            grid,
            grid,
            grid,
            grid,
            grid,
            P(("gx", "gy"), None),
            P(("gx", "gy"), None),
        ),
        out_specs=P(None, None, "gx", "gy", "gz"),
        check_vma=False,
    )
```

```python
import jax
import jax.numpy as jnp
from jax import lax
from jax.experimental import pallas as pl
from jax.experimental.pallas import tpu as pltpu
from jax.sharding import PartitionSpec as P

F32 = jnp.float32
BF16 = jnp.bfloat16
HIGHEST = lax.Precision.HIGHEST
NT = (((1,), (1,)), ((), ()))
NN = (((1,), (0,)), ((), ()))

B, NU, SG, GI, VI, CP = 0, 12, 15, 18, 22, 26
PLANES = 27
GROUP = 32


def faces(axis):
    hi = [(plane, 0) for plane in range(PLANES)]
    hi += [(NU + i, 1) for i in range(3) if i != axis]
    lo = [(plane, 0) for plane in range(PLANES) if plane >= NU or plane % 3 != axis]
    lo = [(plane, layer) for plane, layer in lo if plane != SG + axis]
    return hi, lo


def depth(axis):
    return max(len(face) for face in faces(axis))


def col_lane(zb, k):
    return 252 + k if zb == 3 else 4 * zb + k


def call(body, outs, specs, scratch=(), limit=24):
    return pl.pallas_call(
        body,
        out_shape=[jax.ShapeDtypeStruct(shape, dtype) for shape, dtype in outs],
        in_specs=[pl.BlockSpec(memory_space=space) for space in specs],
        out_specs=[pl.BlockSpec(memory_space=pltpu.VMEM)] * len(outs),
        scratch_shapes=list(scratch),
        compiler_params=pltpu.CompilerParams(vmem_limit_bytes=limit * 1024 * 1024),
    )


def is_even(axis):
    return lax.rem(lax.axis_index(axis), 2) == 0


def send(even, hi, lo, first, second):
    @pl.when(even)
    def _():
        hi(first)
        lo(second)

    @pl.when(jnp.logical_not(even))
    def _():
        hi(second)
        lo(first)


def pack_y(rhs, sign, nu, sigma, gi, vi, cols, own, first, second, rhs_v, sign_v, cols_v, sems):
    copies = [
        pltpu.make_async_copy(rhs, rhs_v, sems.at[0]),
        pltpu.make_async_copy(sign, sign_v, sems.at[1]),
        pltpu.make_async_copy(cols, cols_v, sems.at[2]),
        pltpu.make_async_copy(nu, own.at[NU:SG], sems.at[3]),
        pltpu.make_async_copy(sigma, own.at[SG:GI], sems.at[4]),
        pltpu.make_async_copy(gi, own.at[GI:VI], sems.at[5]),
        pltpu.make_async_copy(vi, own.at[VI:CP], sems.at[6]),
    ]
    for copy in copies:
        copy.start()
    for copy in copies:
        copy.wait()
    lane = lax.broadcasted_iota(jnp.int32, (4, 256), 1)
    for x in range(4):
        plane = jnp.zeros((4, 256), F32)
        for k in range(4):
            for zb in range(4):
                plane = jnp.where(
                    lane == col_lane(zb, k), cols_v[k, x, :, zb : zb + 1].astype(F32), plane
                )
        own[CP, x] = plane
    for i in range(3):
        sign_of = sign_v[i].astype(F32)
        for p in range(4):
            own[3 * p + i] = rhs_v[p, i] * sign_of
    hi_list, lo_list = faces(1)

    def hi(target):
        for at, (plane, layer) in enumerate(hi_list):
            for x in range(4):
                target[at, x : x + 1, :] = own[plane, x, 3 - layer : 4 - layer, :]

    def lo(target):
        for at, (plane, layer) in enumerate(lo_list):
            for x in range(4):
                target[at, x : x + 1, :] = own[plane, x, layer : layer + 1, :]

    send(is_even("gy"), hi, lo, first, second)


def pack_x(own, y_first, y_second, wide, first, second):
    hi_list, lo_list = faces(1)
    hi_at = {entry: at for at, entry in enumerate(hi_list)}
    lo_at = {entry: at for at, entry in enumerate(lo_list)}

    def fill(minus, plus):
        zero = jnp.zeros((1, 256), F32)
        for plane in range(PLANES):
            for x in range(4):
                for row, where, source, key in (
                    (0, hi_at, minus, (plane, 1)),
                    (1, hi_at, minus, (plane, 0)),
                    (6, lo_at, plus, (plane, 0)),
                    (7, lo_at, plus, (plane, 1)),
                ):
                    value = source[where[key], x : x + 1, :] if key in where else zero
                    wide[plane, x, row : row + 1, :] = value
                wide[plane, x, 2:6, :] = own[plane, x]

    even_y = is_even("gy")

    @pl.when(even_y)
    def _():
        fill(y_second, y_first)

    @pl.when(jnp.logical_not(even_y))
    def _():
        fill(y_first, y_second)

    hi_x, lo_x = faces(0)

    def hi(target):
        for at, (plane, layer) in enumerate(hi_x):
            target[at] = wide[plane, 3 - layer]

    def lo(target):
        for at, (plane, layer) in enumerate(lo_x):
            target[at] = wide[plane, layer]

    send(is_even("gx"), hi, lo, first, second)


def slab_source(plane, x):
    hi_x, lo_x = faces(0)
    if 2 <= x < 6:
        return "own", x - 2
    side, entries, layer = ("minus", hi_x, 1 - x) if x < 2 else ("plus", lo_x, x - 6)
    key = (plane, layer)
    return (side, entries.index(key)) if key in entries else (None, None)


def pack_z(wide, x_first, x_second, first, second):
    lane = lax.broadcasted_iota(jnp.int32, (8, 128), 1)

    def fill(minus, plus, hi, lo):
        for x in range(7):
            low = jnp.zeros((8, 128), F32)
            high = jnp.zeros((8, 128), F32)
            for plane in range(PLANES):
                side, at = slab_source(plane, x)
                if side is None:
                    continue
                source = wide.at[plane, at] if side == "own" else (minus if side == "minus" else plus).at[at]
                here = lane // 4 == plane
                low = jnp.where(here, pltpu.roll(source[:, 0:128], 4 * plane, 1), low)
                high = jnp.where(
                    here, pltpu.roll(source[:, 128:256], (4 * plane + 4) % 128, 1), high
                )
            lo[x] = low
            hi[x] = high

    even_x, even_z = is_even("gx"), is_even("gz")
    for x_even in (True, False):
        for z_even in (True, False):

            @pl.when((even_x == x_even) & (even_z == z_even))
            def _(x_even=x_even, z_even=z_even):
                minus, plus = (x_second, x_first) if x_even else (x_first, x_second)
                hi, lo = (first, second) if z_even else (second, first)
                fill(minus, plus, hi, lo)


def ahead(values, axis):
    return pltpu.roll(values, values.shape[axis] - 1, axis)


def behind(values, axis):
    return pltpu.roll(values, 1, axis)


def operate(v0, v1, v2, nu0, nu1, nu2, sg0, sg1, sg2):
    a0, a1, a2 = v0[:5], v1[:5], v2[:5]
    f0 = nu0 * ((ahead(a2, 1) - a2) - (ahead(a1, 2) - a1))
    f1 = nu1 * ((ahead(a0, 2) - a0) - (v2[1:6] - a2))
    f2 = nu2 * ((v1[1:6] - a1) - (ahead(a0, 1) - a0))
    r0 = (behind(f1, 2) - f1) - (behind(f2, 1) - f2) + sg0 * a0
    r1 = (f2[0:4] - f2[1:5]) - (behind(f0, 2)[1:5] - f0[1:5]) + sg1 * v1[1:5]
    r2 = (behind(f0, 1)[1:5] - f0[1:5]) - (f1[0:4] - f1[1:5]) + sg2 * v2[1:5]
    return r0, r1, r2


def restrict(
    wide, x_first, x_second, z_first, z_second, coarse, keep, inverse, ext, base, linv, sums, hot, own_weights
):
    lane = lax.broadcasted_iota(jnp.int32, (8, 128), 1)
    even_x, even_z = is_even("gx"), is_even("gz")

    def place(plane):
        return (base, plane) if plane < NU else (ext, plane - NU)

    def fill(minus, plus):
        zero = jnp.zeros((8, 256), F32)
        for plane in range(PLANES):
            target, to = place(plane)
            for x in (0, 1, 6):
                side, at = slab_source(plane, x)
                value = zero if side is None else (minus if side == "minus" else plus)[at]
                target[to, x, :, 0:256] = value

    @pl.when(even_x)
    def _():
        fill(x_second, x_first)

    @pl.when(jnp.logical_not(even_x))
    def _():
        fill(x_first, x_second)

    base[:, 2:6, :, 0:256] = wide[0:NU]
    ext[:, 2:6, :, 0:256] = wide[NU:PLANES]
    for x in range(7):
        before = jnp.where(even_z, z_second[x], z_first[x])
        after = jnp.where(even_z, z_first[x], z_second[x])
        for plane in range(PLANES):
            target, to = place(plane)
            target[to, x, :, 256:384] = jnp.where(
                lane < 4,
                pltpu.roll(after, (128 - 4 * plane) % 128, 1),
                jnp.where(lane >= 124, pltpu.roll(before, (124 - 4 * plane) % 128, 1), 0.0),
            )
    nu0, nu1, nu2 = ext[0], ext[1], ext[2]
    n0, n1, n2 = nu0[1:7], nu1[1:7], nu2[1:7]
    floor = 0.1
    linv[0] = 1.0 / jnp.maximum(
        ext[3, 1:7] + 4.0 * ((n2 + behind(n2, 1)) + (n1 + behind(n1, 2))), floor
    )
    linv[1] = 1.0 / jnp.maximum(
        ext[4, 1:7] + 4.0 * ((n2 + nu2[0:6]) + (n0 + behind(n0, 2))), floor
    )
    linv[2] = 1.0 / jnp.maximum(
        ext[5, 1:7] + 4.0 * ((n1 + nu1[0:6]) + (n0 + behind(n0, 1))), floor
    )
    for i in range(3):
        inverse[i] = linv[i, 1:5, 2:6, 0:256]
    mine = (lax.axis_index("gx"), lax.axis_index("gy"), lax.axis_index("gz"))
    row = lax.broadcasted_iota(jnp.int32, (8, 256), 0)

    def pair(low, high):
        return jnp.where(row < 4, pltpu.roll(low, 6, 0), pltpu.roll(high, 2, 0))

    for k in range(8):
        for x in range(2):
            own_weights[k, x] = pair(
                ext[GI - NU + k, 2 * x + 2, :, 0:256], ext[GI - NU + k, 2 * x + 3, :, 0:256]
            )
    for x in range(2):
        plane = pair(ext[CP - NU, 2 * x + 2, :, 0:256], ext[CP - NU, 2 * x + 3, :, 0:256])
        for k in range(4):
            column = jnp.zeros((8, 128), F32)
            for zb in range(4):
                at = col_lane(zb, k)
                column = jnp.where(lane // 32 == zb, plane[:, at : at + 1], column)
            node = column.astype(jnp.int32)
            owner = node >> 2
            dx = (owner >> 5) - mine[0]
            dy = ((owner >> 3) & 3) - mine[1]
            dz = (owner & 7) - mine[2]
            side = jnp.where(dx == 1, 1, jnp.where(dx == -1, 2, 0))
            side = jnp.where(dy == 1, 3, jnp.where(dy == -1, 4, side))
            side = jnp.where(dz == 1, 5, jnp.where(dz == -1, 6, side))
            slot = 4 * side + (node & 3)
            at = 16 * k + 8 * x
            hot[at : at + 8] = jnp.where(slot == lane % 32, 1.0, 0.0)
    pick = (
        lax.broadcasted_iota(jnp.int32, (256, 128), 0) // 64
        == lax.broadcasted_iota(jnp.int32, (256, 128), 1) // 32
    )
    pick = jnp.where(pick, 1.0, 0.0).astype(BF16)

    def port(p):
        b0, b1, b2 = base[3 * p], base[3 * p + 1], base[3 * p + 2]
        u0, u1, u2 = b0[1:6] * linv[0, 0:5], b1[1:7] * linv[1], b2[1:7] * linv[2]
        r0, r1, r2 = operate(
            u0, u1, u2, ext[0, 1:6], ext[1, 1:6], ext[2, 1:6], ext[3, 1:6], ext[4, 2:6], ext[5, 2:6]
        )
        t0, t1, t2 = b0[1:6] - r0, b1[2:6] - r1, b2[2:6] - r2
        here = (t0[1:5], t1, t2)
        back = (t0[0:4], behind(t1, 1), behind(t2, 2))
        wide_u = (u0, u1, u2)
        parts = [((back[0] - here[0]) + (back[1] - here[1])) + (back[2] - here[2])]
        for i in range(3):
            kept = wide_u[i][1:5] + here[i] * linv[i, 1:5]
            keep[3 * p + i] = kept[:, 2:6, 0:256]
            parts.append(0.5 * (here[i] + back[i]))
        for kind in range(4):
            first = 0 if kind == 0 else 4
            part = parts[kind][:, :, 0:256]
            pairs = [pair(part[0], part[1]), pair(part[2], part[3])]
            products = [pairs[x] * own_weights[first + k, x] for k in range(4) for x in range(2)]
            product = jnp.concatenate(products, 0)
            top = product.astype(BF16)
            middle = (product - top.astype(F32)).astype(BF16)
            blocks = jnp.dot(top, pick, preferred_element_type=F32) + jnp.dot(
                middle, pick, preferred_element_type=F32
            )
            total = jnp.sum((blocks * hot[...]).reshape(8, 8, 128), axis=0)
            sums[4 * kind + p] = total

    for p in range(4):
        port(p)

    total = jnp.sum(sums[...], axis=1)
    total = total + pltpu.roll(total, 64, 1)
    total = total + pltpu.roll(total, 32, 1)
    quarter = lax.broadcasted_iota(jnp.int32, (4, 128), 1) // 32
    mixed = total[0:4]
    for kind in range(1, 4):
        mixed = jnp.where(quarter == kind, total[4 * kind : 4 * kind + 4], mixed)
    for g in range(GROUP):
        coarse[g] = mixed


def multiply(parts, grad_rows, vec_rows, out, stacked):
    for gx in range(8):
        for gy in range(4):
            for kind in range(4):
                stacked[16 * gx + 4 * kind : 16 * gx + 4 * kind + 4, 32 * gy : 32 * gy + 32] = parts[
                    4 * gx + gy, :, 32 * kind : 32 * kind + 32
                ]
    z = lax.axis_index("gz")
    row = lax.broadcasted_iota(jnp.int32, (128, 128), 0)
    lane = lax.broadcasted_iota(jnp.int32, (128, 128), 1)
    gy = row // 32
    side = (row % 32) >> 2
    gy_to = gy + jnp.where(side == 3, 1, 0) - jnp.where(side == 4, 1, 0)
    z_to = z + jnp.where(side == 5, 1, 0) - jnp.where(side == 6, 1, 0)
    hit = lane == 32 * gy_to + 4 * z_to + (row & 3)
    stay = jnp.where(hit & ((side == 0) | ((side >= 3) & (side <= 6))), 1.0, 0.0)
    forth = jnp.where(hit & (side == 1), 1.0, 0.0)
    back = jnp.where(hit & (side == 2), 1.0, 0.0)

    def spread(where):
        return lax.dot_general(
            stacked[...], where, NN, precision=HIGHEST, preferred_element_type=F32
        )

    stays, forths, backs = spread(stay), spread(forth), spread(back)
    tiles = []
    for gx in range(8):
        tile = stays[16 * gx : 16 * gx + 16]
        if gx > 0:
            tile = tile + forths[16 * gx - 16 : 16 * gx]
        if gx < 7:
            tile = tile + backs[16 * gx + 16 : 16 * gx + 32]
        tiles.append(tile)
    vector = jnp.concatenate(tiles, 1)
    grad = lax.dot_general(
        vector[0:8], grad_rows[...], NT, precision=HIGHEST, preferred_element_type=F32
    )[0:4]
    vec = jnp.zeros((4, 96), F32)
    for i in range(3):
        start = 4 + 4 * i
        half = 8 * (start // 8)
        product = lax.dot_general(
            vector[half : half + 8],
            vec_rows[:, 1024 * i : 1024 * i + 1024],
            NT,
            precision=HIGHEST,
            preferred_element_type=F32,
        )
        vec = vec + product[start - half : start - half + 4]
    for z_at in range(8):
        out[z_at, :, 0:32] = grad
        out[z_at, :, 32:128] = vec


def finish(values, ext, keep, inverse, sign, out, dense, nodal):
    gx = lax.axis_index("gx")
    for tile in (0, 1, 10, 11):
        dense[tile] = jnp.zeros((16, 128), F32)
    for g in range(GROUP):
        at = 32 * (g % 4)
        dense[2 + g // 4, 0:4, at : at + 32] = values[g, :, 0:32]
        for c in range(3):
            q = 3 * g + c
            row = 4 + 4 * (q // 32)
            tile, at = 2 + (q % 32) // 4, 32 * (q % 4)
            dense[tile, row : row + 4, at : at + 32] = values[g, :, 32 + 32 * c : 64 + 32 * c]
    whole = jnp.concatenate([dense[gx + tile] for tile in range(5)], 1)
    top = whole.astype(BF16)
    rest = whole - top.astype(F32)
    middle = rest.astype(BF16)
    bottom = (rest - middle.astype(F32)).astype(BF16)
    split = jnp.concatenate([top, middle, bottom], 0)
    blank = jnp.zeros((48, 640), BF16)
    sides = (jnp.concatenate([split, blank], 0), jnp.concatenate([blank, split], 0))
    select_row = lax.broadcasted_iota(jnp.int32, (96, 2048), 0)
    select_lane = lax.broadcasted_iota(jnp.int32, (96, 2048), 1)
    select = jnp.where(
        ((select_row % 16) == (select_lane // 128))
        & ((select_row // 48) == ((select_lane // 64) % 2)),
        1.0,
        0.0,
    ).astype(BF16)
    node = lax.broadcasted_iota(jnp.int32, (8, 640), 1) + 128 * (gx - 2)
    lanes = (
        [col_lane(0, k) for k in range(4)],
        [col_lane(1, k) for k in range(4)],
        [col_lane(2, k) for k in range(4)],
        [col_lane(3, k) for k in range(4)],
        [256 + k for k in range(4)],
        [380 + k for k in range(4)],
    )
    for tile in range(3):
        taken = jnp.zeros((192, 96), F32)
        for half in range(2):
            rows = []
            for k in range(4):
                at = lanes[2 * tile + half][k]
                for x in range(1, 7):
                    column = ext[CP - NU, x, :, at : at + 1].astype(jnp.int32)
                    rows.append(jnp.where(column == node, 1.0, 0.0).astype(F32))
            hot = jnp.concatenate(rows, 0).astype(BF16)
            taken = taken + lax.dot_general(hot, sides[half], NT, preferred_element_type=F32)
        taken = taken.astype(BF16)
        for kind in range(4):
            first = GI - NU if kind == 0 else VI - NU
            spread = lax.dot_general(
                taken,
                select[:, 512 * kind : 512 * kind + 512],
                NN,
                preferred_element_type=F32,
            )
            for p in range(4):
                total = jnp.zeros((6, 8, 128), F32)
                for k in range(4):
                    total = total + ext[first + k, 1:7, :, 128 * tile : 128 * tile + 128] * spread[
                        48 * k : 48 * k + 48, 128 * p : 128 * p + 128
                    ].reshape(6, 8, 128)
                nodal[4 * kind + p, :, :, 128 * tile : 128 * tile + 128] = total

    shape = (6, 8, 384)
    x_at = lax.broadcasted_iota(jnp.int32, shape, 0)
    y_at = lax.broadcasted_iota(jnp.int32, shape, 1)
    z_at = lax.broadcasted_iota(jnp.int32, shape, 2)
    outside_x = (x_at == 0) & (lax.axis_index("gx") == 0)
    outside_y = (y_at == 1) & (lax.axis_index("gy") == 0)
    outside_z = (z_at == 383) & (lax.axis_index("gz") == 0)

    def port(p):
        g = nodal[p]
        v0, v1, v2 = nodal[4 + p], nodal[8 + p], nodal[12 + p]
        c0 = (g[1:6] - g[0:5]) + 0.5 * (v0[0:5] + v0[1:6])
        c1 = (ahead(g, 1) - g) + 0.5 * (v1 + ahead(v1, 1))
        c2 = (ahead(g, 2) - g) + 0.5 * (v2 + ahead(v2, 2))
        c0 = jnp.where(outside_x[0:5], 0.0, c0)
        c1 = jnp.where(outside_y, 0.0, c1)
        c2 = jnp.where(outside_z, 0.0, c2)
        r0, r1, r2 = operate(
            c0, c1, c2, ext[0, 1:6], ext[1, 1:6], ext[2, 1:6], ext[3, 1:6], ext[4, 2:6], ext[5, 2:6]
        )
        fields = ((c0[1:5], r0[1:5]), (c1[1:5], r1), (c2[1:5], r2))
        for i in range(3):
            c, r = fields[i]
            w = keep[3 * p + i] + (c[:, 2:6, 0:256] - r[:, 2:6, 0:256] * inverse[i])
            out[p, i] = sign[i].astype(F32) * w

    for p in range(4):
        port(p)


def exchange(first, second, axis):
    count = lax.axis_size(axis)

    def pairs(start):
        found = []
        for i in range(start, count - 1, 2):
            found += [(i, i + 1), (i + 1, i)]
        return found

    return lax.ppermute(first, axis, pairs(0)), lax.ppermute(second, axis, pairs(1))


def per_device(rhs, sign, nu, sigma, cols, gi, vi, grad_rows, vec_rows):
    vmem = pltpu.VMEM
    own, first, second = call(
        pack_y,
        [((PLANES, 4, 4, 256), F32)] + [((depth(1), 4, 256), F32)] * 2,
        [pl.ANY] * 7,
        [
            pltpu.VMEM((4, 3, 4, 4, 256), F32),
            pltpu.VMEM((3, 4, 4, 256), jnp.int32),
            pltpu.VMEM((4, 4, 4, 4), jnp.int32),
            pltpu.SemaphoreType.DMA((7,)),
        ],
    )(*[pltpu.with_memory_space_constraint(x, pltpu.HBM) for x in (rhs, sign, nu, sigma, gi, vi, cols)])
    first, second = exchange(first, second, "gy")
    wide, x_first, x_second = call(
        pack_x,
        [((PLANES, 4, 8, 256), F32)] + [((depth(0), 8, 256), F32)] * 2,
        [vmem] * 3,
    )(own, first, second)
    x_first, x_second = exchange(x_first, x_second, "gx")
    z_first, z_second = call(pack_z, [((7, 8, 128), F32)] * 2, [vmem] * 3)(
        wide, x_first, x_second
    )
    z_first, z_second = exchange(z_first, z_second, "gz")
    coarse, keep, inverse, ext = call(
        restrict,
        [
            ((GROUP, 4, 128), F32),
            ((12, 4, 4, 256), F32),
            ((3, 4, 4, 256), F32),
            ((PLANES - NU, 7, 8, 384), F32),
        ],
        [vmem] * 5,
        [
            pltpu.VMEM((NU, 7, 8, 384), F32),
            pltpu.VMEM((3, 6, 8, 384), F32),
            pltpu.VMEM((16, 8, 128), F32),
            pltpu.VMEM((64, 128), F32),
            pltpu.VMEM((8, 2, 8, 256), F32),
        ],
    )(wide, x_first, x_second, z_first, z_second)
    coarse = lax.all_to_all(coarse, ("gx", "gy"), 0, 0)
    (partial,) = call(
        multiply, [((8, 4, 128), F32)], [vmem] * 3, [pltpu.VMEM((128, 128), F32)]
    )(coarse, grad_rows, vec_rows)
    partial = lax.all_to_all(partial, "gz", 0, 0)
    values = jnp.broadcast_to(jnp.sum(partial, 0)[None], (GROUP, 4, 128))
    values = lax.all_to_all(values, ("gx", "gy"), 0, 0)
    (out,) = call(
        finish,
        [((4, 3, 4, 4, 256), F32)],
        [vmem] * 5,
        [pltpu.VMEM((12, 16, 128), F32), pltpu.VMEM((16, 6, 8, 384), F32)],
    )(values, ext, keep, inverse, sign)
    return out


def solution(mesh):
    grid = P(None, "gx", "gy", "gz")
    return jax.shard_map(
        per_device,
        mesh=mesh,
        in_specs=(
            P(None, None, "gx", "gy", "gz"),
            grid,
            grid,
            grid,
            grid,
            grid,
            grid,
            P(("gx", "gy"), None),
            P(("gx", "gy"), None),
        ),
        out_specs=P(None, None, "gx", "gy", "gz"),
        check_vma=False,
    )
```

```python
import jax
import jax.numpy as jnp
from jax import lax
from jax.experimental import pallas as pl
from jax.experimental.pallas import tpu as pltpu
from jax.sharding import PartitionSpec as P

F32 = jnp.float32
BF16 = jnp.bfloat16
HIGHEST = lax.Precision.HIGHEST
NT = (((1,), (1,)), ((), ()))
NN = (((1,), (0,)), ((), ()))

B, NU, SG, GI, VI, CP = 0, 12, 15, 18, 22, 26
PLANES = 27
GROUP = 32


def faces(axis):
    hi = [(plane, 0) for plane in range(PLANES)]
    hi += [(NU + i, 1) for i in range(3) if i != axis]
    lo = [(plane, 0) for plane in range(PLANES) if plane >= NU or plane % 3 != axis]
    lo = [(plane, layer) for plane, layer in lo if plane != SG + axis]
    return hi, lo


def depth(axis):
    return max(len(face) for face in faces(axis))


def col_lane(zb, k):
    return 252 + k if zb == 3 else 4 * zb + k


def call(body, outs, specs, scratch=(), limit=12, cost=None):
    return pl.pallas_call(
        body,
        out_shape=[jax.ShapeDtypeStruct(shape, dtype) for shape, dtype in outs],
        in_specs=[pl.BlockSpec(memory_space=space) for space in specs],
        out_specs=[pl.BlockSpec(memory_space=pltpu.VMEM)] * len(outs),
        scratch_shapes=list(scratch),
        cost_estimate=cost and pl.CostEstimate(flops=cost[0], bytes_accessed=cost[1], transcendentals=0),
        compiler_params=pltpu.CompilerParams(vmem_limit_bytes=limit * 1024 * 1024),
    )


def in_hbm(x):
    return pltpu.with_memory_space_constraint(x, pltpu.HBM)


def is_even(axis):
    return lax.rem(lax.axis_index(axis), 2) == 0


def send(even, hi, lo, first, second):
    @pl.when(even)
    def _():
        hi(first)
        lo(second)

    @pl.when(jnp.logical_not(even))
    def _():
        hi(second)
        lo(first)


def pack_y(rhs, sign, nu, sigma, gi, vi, cols, own, first, second, rhs_v, sign_v, cols_v, sems):
    copies = [
        pltpu.make_async_copy(rhs, rhs_v, sems.at[0]),
        pltpu.make_async_copy(sign, sign_v, sems.at[1]),
        pltpu.make_async_copy(cols, cols_v, sems.at[2]),
        pltpu.make_async_copy(nu, own.at[NU:SG], sems.at[3]),
        pltpu.make_async_copy(sigma, own.at[SG:GI], sems.at[4]),
        pltpu.make_async_copy(gi, own.at[GI:VI], sems.at[5]),
        pltpu.make_async_copy(vi, own.at[VI:CP], sems.at[6]),
    ]
    for copy in copies:
        copy.start()
    for copy in copies:
        copy.wait()
    lane = lax.broadcasted_iota(jnp.int32, (4, 256), 1)
    for x in range(4):
        plane = jnp.zeros((4, 256), F32)
        for k in range(4):
            for zb in range(4):
                plane = jnp.where(
                    lane == col_lane(zb, k), cols_v[k, x, :, zb : zb + 1].astype(F32), plane
                )
        own[CP, x] = plane
    for i in range(3):
        sign_of = sign_v[i].astype(F32)
        for p in range(4):
            own[3 * p + i] = rhs_v[p, i] * sign_of
    hi_list, lo_list = faces(1)

    def hi(target):
        for at, (plane, layer) in enumerate(hi_list):
            for x in range(4):
                target[at, x : x + 1, :] = own[plane, x, 3 - layer : 4 - layer, :]

    def lo(target):
        for at, (plane, layer) in enumerate(lo_list):
            for x in range(4):
                target[at, x : x + 1, :] = own[plane, x, layer : layer + 1, :]

    send(is_even("gy"), hi, lo, first, second)


def pack_x(own, y_second, y_first, wide, first, second):
    hi_list, lo_list = faces(1)
    hi_at = {entry: at for at, entry in enumerate(hi_list)}
    lo_at = {entry: at for at, entry in enumerate(lo_list)}

    def fill(minus, plus):
        zero = jnp.zeros((1, 256), F32)
        for plane in range(PLANES):
            for x in range(4):
                for row, where, source, key in (
                    (0, hi_at, minus, (plane, 1)),
                    (1, hi_at, minus, (plane, 0)),
                    (6, lo_at, plus, (plane, 0)),
                    (7, lo_at, plus, (plane, 1)),
                ):
                    value = source[where[key], x : x + 1, :] if key in where else zero
                    wide[plane, x, row : row + 1, :] = value
                wide[plane, x, 2:6, :] = own[plane, x]

    even_y = is_even("gy")

    @pl.when(even_y)
    def _():
        fill(y_second, y_first)

    @pl.when(jnp.logical_not(even_y))
    def _():
        fill(y_first, y_second)

    hi_x, lo_x = faces(0)

    def hi(target):
        for at, (plane, layer) in enumerate(hi_x):
            target[at] = wide[plane, 3 - layer]

    def lo(target):
        for at, (plane, layer) in enumerate(lo_x):
            target[at] = wide[plane, layer]

    send(is_even("gx"), hi, lo, first, second)


def slab_source(plane, x):
    hi_x, lo_x = faces(0)
    if 2 <= x < 6:
        return "own", x - 2
    side, entries, layer = ("minus", hi_x, 1 - x) if x < 2 else ("plus", lo_x, x - 6)
    key = (plane, layer)
    return (side, entries.index(key)) if key in entries else (None, None)


def pack_z(wide, x_first, x_second, after, first, second):
    lane = lax.broadcasted_iota(jnp.int32, (8, 128), 1)

    def fill(minus, plus, hi, lo):
        for x in range(7):
            low = jnp.zeros((8, 128), F32)
            high = jnp.zeros((8, 128), F32)
            for plane in range(PLANES):
                side, at = slab_source(plane, x)
                if side is None:
                    continue
                source = wide.at[plane, at] if side == "own" else (minus if side == "minus" else plus).at[at]
                here = lane // 4 == plane
                low = jnp.where(here, pltpu.roll(source[:, 0:128], 4 * plane, 1), low)
                high = jnp.where(
                    here, pltpu.roll(source[:, 128:256], (4 * plane + 4) % 128, 1), high
                )
            lo[x] = low
            hi[x] = high

    even_x, even_z = is_even("gx"), is_even("gz")
    for x_even in (True, False):
        for z_even in (True, False):

            @pl.when((even_x == x_even) & (even_z == z_even))
            def _(x_even=x_even, z_even=z_even):
                minus, plus = (x_second, x_first) if x_even else (x_first, x_second)
                hi, lo = (first, second) if z_even else (second, first)
                fill(minus, plus, hi, lo)


def ahead(values, axis):
    return pltpu.roll(values, values.shape[axis] - 1, axis)


def behind(values, axis):
    return pltpu.roll(values, 1, axis)


def operate(v0, v1, v2, nu0, nu1, nu2, sg0, sg1, sg2):
    a0, a1, a2 = v0[:5], v1[:5], v2[:5]
    f0 = nu0 * ((ahead(a2, 1) - a2) - (ahead(a1, 2) - a1))
    f1 = nu1 * ((ahead(a0, 2) - a0) - (v2[1:6] - a2))
    f2 = nu2 * ((v1[1:6] - a1) - (ahead(a0, 1) - a0))
    r0 = (behind(f1, 2) - f1) - (behind(f2, 1) - f2) + sg0 * a0
    r1 = (f2[0:4] - f2[1:5]) - (behind(f0, 2)[1:5] - f0[1:5]) + sg1 * v1[1:5]
    r2 = (behind(f0, 1)[1:5] - f0[1:5]) - (f1[0:4] - f1[1:5]) + sg2 * v2[1:5]
    return r0, r1, r2


def restrict(
    wide, x_first, x_second, z_second, z_first, coarse, keep, inverse, ext, base, linv, sums, hot, own_weights
):
    lane = lax.broadcasted_iota(jnp.int32, (8, 128), 1)
    even_x, even_z = is_even("gx"), is_even("gz")

    def place(plane):
        return (base, plane) if plane < NU else (ext, plane - NU)

    def fill(minus, plus):
        zero = jnp.zeros((8, 256), F32)
        for plane in range(PLANES):
            target, to = place(plane)
            for x in (0, 1, 6):
                side, at = slab_source(plane, x)
                value = zero if side is None else (minus if side == "minus" else plus)[at]
                target[to, x, :, 0:256] = value

    @pl.when(even_x)
    def _():
        fill(x_second, x_first)

    @pl.when(jnp.logical_not(even_x))
    def _():
        fill(x_first, x_second)

    base[:, 2:6, :, 0:256] = wide[0:NU]
    ext[:, 2:6, :, 0:256] = wide[NU:PLANES]
    for x in range(7):
        before = jnp.where(even_z, z_second[x], z_first[x])
        after = jnp.where(even_z, z_first[x], z_second[x])
        for plane in range(PLANES):
            target, to = place(plane)
            target[to, x, :, 256:384] = jnp.where(
                lane < 4,
                pltpu.roll(after, (128 - 4 * plane) % 128, 1),
                jnp.where(lane >= 124, pltpu.roll(before, (124 - 4 * plane) % 128, 1), 0.0),
            )
    nu0, nu1, nu2 = ext[0], ext[1], ext[2]
    n0, n1, n2 = nu0[1:7], nu1[1:7], nu2[1:7]
    floor = 0.1
    linv[0] = 1.0 / jnp.maximum(
        ext[3, 1:7] + 4.0 * ((n2 + behind(n2, 1)) + (n1 + behind(n1, 2))), floor
    )
    linv[1] = 1.0 / jnp.maximum(
        ext[4, 1:7] + 4.0 * ((n2 + nu2[0:6]) + (n0 + behind(n0, 2))), floor
    )
    linv[2] = 1.0 / jnp.maximum(
        ext[5, 1:7] + 4.0 * ((n1 + nu1[0:6]) + (n0 + behind(n0, 1))), floor
    )
    for i in range(3):
        inverse[i] = linv[i, 1:5, 2:6, 0:256]
    mine = (lax.axis_index("gx"), lax.axis_index("gy"), lax.axis_index("gz"))
    row = lax.broadcasted_iota(jnp.int32, (8, 256), 0)

    def pair(low, high):
        return jnp.where(row < 4, pltpu.roll(low, 6, 0), pltpu.roll(high, 2, 0))

    for k in range(8):
        for x in range(2):
            own_weights[k, x] = pair(
                ext[GI - NU + k, 2 * x + 2, :, 0:256], ext[GI - NU + k, 2 * x + 3, :, 0:256]
            )
    for x in range(2):
        plane = pair(ext[CP - NU, 2 * x + 2, :, 0:256], ext[CP - NU, 2 * x + 3, :, 0:256])
        for k in range(4):
            column = jnp.zeros((8, 128), F32)
            for zb in range(4):
                at = col_lane(zb, k)
                column = jnp.where(lane // 32 == zb, plane[:, at : at + 1], column)
            node = column.astype(jnp.int32)
            owner = node >> 2
            dx = (owner >> 5) - mine[0]
            dy = ((owner >> 3) & 3) - mine[1]
            dz = (owner & 7) - mine[2]
            side = jnp.where(dx == 1, 1, jnp.where(dx == -1, 2, 0))
            side = jnp.where(dy == 1, 3, jnp.where(dy == -1, 4, side))
            side = jnp.where(dz == 1, 5, jnp.where(dz == -1, 6, side))
            slot = 4 * side + (node & 3)
            at = 16 * k + 8 * x
            hot[at : at + 8] = jnp.where(slot == lane % 32, 1.0, 0.0)
    pick = (
        lax.broadcasted_iota(jnp.int32, (256, 128), 0) // 64
        == lax.broadcasted_iota(jnp.int32, (256, 128), 1) // 32
    )
    pick = jnp.where(pick, 1.0, 0.0).astype(BF16)

    def port(p):
        b0, b1, b2 = base[3 * p], base[3 * p + 1], base[3 * p + 2]
        u0, u1, u2 = b0[1:6] * linv[0, 0:5], b1[1:7] * linv[1], b2[1:7] * linv[2]
        r0, r1, r2 = operate(
            u0, u1, u2, ext[0, 1:6], ext[1, 1:6], ext[2, 1:6], ext[3, 1:6], ext[4, 2:6], ext[5, 2:6]
        )
        t0, t1, t2 = b0[1:6] - r0, b1[2:6] - r1, b2[2:6] - r2
        here = (t0[1:5], t1, t2)
        back = (t0[0:4], behind(t1, 1), behind(t2, 2))
        wide_u = (u0, u1, u2)
        parts = [((back[0] - here[0]) + (back[1] - here[1])) + (back[2] - here[2])]
        for i in range(3):
            kept = wide_u[i][1:5] + here[i] * linv[i, 1:5]
            keep[3 * p + i] = kept[:, 2:6, 0:256]
            parts.append(0.5 * (here[i] + back[i]))
        for kind in range(4):
            first = 0 if kind == 0 else 4
            part = parts[kind][:, :, 0:256]
            pairs = [pair(part[0], part[1]), pair(part[2], part[3])]
            products = [pairs[x] * own_weights[first + k, x] for k in range(4) for x in range(2)]
            product = jnp.concatenate(products, 0)
            top = product.astype(BF16)
            middle = (product - top.astype(F32)).astype(BF16)
            blocks = jnp.dot(top, pick, preferred_element_type=F32) + jnp.dot(
                middle, pick, preferred_element_type=F32
            )
            total = jnp.sum((blocks * hot[...]).reshape(8, 8, 128), axis=0)
            sums[4 * kind + p] = total

    for p in range(4):
        port(p)

    total = jnp.sum(sums[...], axis=1)
    total = total + pltpu.roll(total, 64, 1)
    total = total + pltpu.roll(total, 32, 1)
    quarter = lax.broadcasted_iota(jnp.int32, (4, 128), 1) // 32
    mixed = total[0:4]
    for kind in range(1, 4):
        mixed = jnp.where(quarter == kind, total[4 * kind : 4 * kind + 4], mixed)
    for g in range(GROUP):
        coarse[g] = mixed


def parts_of(value):
    top = value.astype(BF16)
    rest = value - top.astype(F32)
    middle = rest.astype(BF16)
    bottom = (rest - middle.astype(F32)).astype(BF16)
    return top, middle, bottom


def prepare(
    grad_hbm, vec_hbm, after, grad_parts, vec_parts, spread, select, grad_rows, vec_rows, sems
):
    copies = (
        pltpu.make_async_copy(grad_hbm, grad_rows, sems.at[0]),
        pltpu.make_async_copy(vec_hbm, vec_rows, sems.at[1]),
    )
    for copy in copies:
        copy.start()
    for copy in copies:
        copy.wait()
    for at, part in enumerate(parts_of(grad_rows[...])):
        grad_parts[at] = part
    for i in range(3):
        columns = pl.ds(1024 * i, 1024)
        for at, part in enumerate(parts_of(vec_rows[:, columns])):
            vec_parts[at, :, columns] = part
    z = lax.axis_index("gz")
    row = lax.broadcasted_iota(jnp.int32, (128, 128), 0)
    lane = lax.broadcasted_iota(jnp.int32, (128, 128), 1)
    gy = row >> 5
    side = (row & 31) >> 2
    gy_to = gy + jnp.where(side == 3, 1, 0) - jnp.where(side == 4, 1, 0)
    z_to = z + jnp.where(side == 5, 1, 0) - jnp.where(side == 6, 1, 0)
    hit = lane == 32 * gy_to + 4 * z_to + (row & 3)
    stay = hit & ((side == 0) | ((side >= 3) & (side <= 6)))
    for at, where in enumerate((stay, hit & (side == 1), hit & (side == 2))):
        spread[:, 128 * at : 128 * at + 128] = jnp.where(where, 1.0, 0.0).astype(BF16)
    row = lax.broadcasted_iota(jnp.int32, (96, 128), 0)
    lane = lax.broadcasted_iota(jnp.int32, (96, 128), 1)
    half = jnp.where((row >= 48) == (lane >= 64), 1.0, 0.0)
    for at in range(16):
        select[:, 128 * at : 128 * at + 128] = jnp.where((row & 15) == at, half, 0.0).astype(BF16)


def multiply(parts, grad_parts, vec_parts, spread, out, stacked):
    for gx in range(8):
        for gy in range(4):
            for kind in range(4):
                stacked[16 * gx + 4 * kind : 16 * gx + 4 * kind + 4, 32 * gy : 32 * gy + 32] = parts[
                    4 * gx + gy, :, 32 * kind : 32 * kind + 32
                ]
    moved = jnp.dot(
        jnp.concatenate(parts_of(stacked[...]), 0), spread[...], preferred_element_type=F32
    )
    moved = (moved[0:128] + moved[128:256]) + moved[256:384]
    tiles = []
    for gx in range(8):
        tile = moved[16 * gx : 16 * gx + 16, 0:128]
        if gx > 0:
            tile = tile + moved[16 * gx - 16 : 16 * gx, 128:256]
        if gx < 7:
            tile = tile + moved[16 * gx + 16 : 16 * gx + 32, 256:384]
        tiles.append(tile)
    vector = jnp.concatenate(tiles, 1)
    top, middle, bottom = (part.astype(F32) for part in parts_of(vector))

    def rows_of(kind):
        at = 4 * kind
        pieces = [part[at : at + 4] for part in (top, middle, bottom)]
        return jnp.concatenate(pieces + [jnp.zeros((4, 1024), F32)], 0).astype(BF16)

    def gathered(products):
        first, second, third = products
        small = third[0:4] + second[4:8] + first[8:12]
        return (small + (second[0:4] + first[4:8])) + first[0:4]

    def product(rows, weights):
        return lax.dot_general(rows, weights, NT, preferred_element_type=F32)

    rows = [rows_of(kind) for kind in range(4)]
    grad = gathered([product(rows[0], grad_parts[at]) for at in range(3)])
    vec = gathered(
        [
            sum(
                product(rows[1 + i], vec_parts[at, :, 1024 * i : 1024 * i + 1024])
                for i in range(3)
            )
            for at in range(3)
        ]
    )
    for z_at in range(8):
        out[z_at, :, 0:32] = grad
        out[z_at, :, 32:128] = vec


def finish(values, ext, keep, inverse, sign, select, out, dense, nodal):
    gx = lax.axis_index("gx")
    for tile in (0, 1, 10, 11):
        dense[tile] = jnp.zeros((16, 128), F32)
    for g in range(GROUP):
        at = 32 * (g % 4)
        dense[2 + g // 4, 0:4, at : at + 32] = values[g, :, 0:32]
        for c in range(3):
            q = 3 * g + c
            row = 4 + 4 * (q // 32)
            tile, at = 2 + (q % 32) // 4, 32 * (q % 4)
            dense[tile, row : row + 4, at : at + 32] = values[g, :, 32 + 32 * c : 64 + 32 * c]
    whole = jnp.concatenate([dense[gx + tile] for tile in range(5)], 1)
    split = jnp.concatenate(parts_of(whole), 0)
    blank = jnp.zeros((48, 640), BF16)
    sides = (jnp.concatenate([split, blank], 0), jnp.concatenate([blank, split], 0))
    node = lax.broadcasted_iota(jnp.int32, (8, 640), 1) + 128 * (gx - 2)
    lanes = (
        [col_lane(0, k) for k in range(4)],
        [col_lane(1, k) for k in range(4)],
        [col_lane(2, k) for k in range(4)],
        [col_lane(3, k) for k in range(4)],
        [256 + k for k in range(4)],
        [380 + k for k in range(4)],
    )
    for tile in range(3):
        taken = jnp.zeros((192, 96), F32)
        for half in range(2):
            rows = []
            for k in range(4):
                at = lanes[2 * tile + half][k]
                for x in range(1, 7):
                    column = ext[CP - NU, x, :, at : at + 1].astype(jnp.int32)
                    rows.append(jnp.where(column == node, 1.0, 0.0).astype(F32))
            hot = jnp.concatenate(rows, 0).astype(BF16)
            taken = taken + lax.dot_general(hot, sides[half], NT, preferred_element_type=F32)
        taken = taken.astype(BF16)
        for kind in range(4):
            first = GI - NU if kind == 0 else VI - NU
            spread = lax.dot_general(
                taken,
                select[:, 512 * kind : 512 * kind + 512],
                NN,
                preferred_element_type=F32,
            )
            for p in range(4):
                total = jnp.zeros((6, 8, 128), F32)
                for k in range(4):
                    total = total + ext[first + k, 1:7, :, 128 * tile : 128 * tile + 128] * spread[
                        48 * k : 48 * k + 48, 128 * p : 128 * p + 128
                    ].reshape(6, 8, 128)
                nodal[4 * kind + p, :, :, 128 * tile : 128 * tile + 128] = total

    shape = (6, 8, 384)
    x_at = lax.broadcasted_iota(jnp.int32, shape, 0)
    y_at = lax.broadcasted_iota(jnp.int32, shape, 1)
    z_at = lax.broadcasted_iota(jnp.int32, shape, 2)
    outside_x = (x_at == 0) & (lax.axis_index("gx") == 0)
    outside_y = (y_at == 1) & (lax.axis_index("gy") == 0)
    outside_z = (z_at == 383) & (lax.axis_index("gz") == 0)

    def port(p):
        g = nodal[p]
        v0, v1, v2 = nodal[4 + p], nodal[8 + p], nodal[12 + p]
        c0 = (g[1:6] - g[0:5]) + 0.5 * (v0[0:5] + v0[1:6])
        c1 = (ahead(g, 1) - g) + 0.5 * (v1 + ahead(v1, 1))
        c2 = (ahead(g, 2) - g) + 0.5 * (v2 + ahead(v2, 2))
        c0 = jnp.where(outside_x[0:5], 0.0, c0)
        c1 = jnp.where(outside_y, 0.0, c1)
        c2 = jnp.where(outside_z, 0.0, c2)
        r0, r1, r2 = operate(
            c0, c1, c2, ext[0, 1:6], ext[1, 1:6], ext[2, 1:6], ext[3, 1:6], ext[4, 2:6], ext[5, 2:6]
        )
        fields = ((c0[1:5], r0[1:5]), (c1[1:5], r1), (c2[1:5], r2))
        for i in range(3):
            c, r = fields[i]
            w = keep[3 * p + i] + (c[:, 2:6, 0:256] - r[:, 2:6, 0:256] * inverse[i])
            out[p, i] = sign[i].astype(F32) * w

    for p in range(4):
        port(p)


def exchange(first, second, axis):
    count = lax.axis_size(axis)

    def pairs(start):
        found = []
        for i in range(start, count - 1, 2):
            found += [(i, i + 1), (i + 1, i)]
        return found

    return lax.ppermute(first, axis, pairs(0)), lax.ppermute(second, axis, pairs(1))


def per_device(rhs, sign, nu, sigma, cols, gi, vi, grad_rows, vec_rows):
    vmem = pltpu.VMEM
    own, first, second = call(
        pack_y,
        [((PLANES, 4, 4, 256), F32)] + [((depth(1), 4, 256), F32)] * 2,
        [pl.ANY] * 7,
        [
            pltpu.VMEM((4, 3, 4, 4, 256), F32),
            pltpu.VMEM((3, 4, 4, 256), jnp.int32),
            pltpu.VMEM((4, 4, 4, 4), jnp.int32),
            pltpu.SemaphoreType.DMA((7,)),
        ],
    )(*[in_hbm(x) for x in (rhs, sign, nu, sigma, gi, vi, cols)])
    first, second = exchange(first, second, "gy")
    wide, x_first, x_second = call(
        pack_x,
        [((PLANES, 4, 8, 256), F32)] + [((depth(0), 8, 256), F32)] * 2,
        [vmem] * 3,
    )(own, second, first)
    grad_parts, vec_parts, spread, select = call(
        prepare,
        [((3, 32, 1024), BF16), ((3, 96, 3072), BF16), ((128, 384), BF16), ((96, 2048), BF16)],
        [pl.ANY] * 3,
        [
            pltpu.VMEM((32, 1024), F32),
            pltpu.VMEM((96, 3072), F32),
            pltpu.SemaphoreType.DMA((2,)),
        ],
        cost=(0, 8_000_000),
    )(in_hbm(grad_rows), in_hbm(vec_rows), x_first)
    x_first, x_second = exchange(x_first, x_second, "gx")
    z_first, z_second = call(pack_z, [((7, 8, 128), F32)] * 2, [vmem] * 3 + [pl.ANY])(
        wide, x_first, x_second, select
    )
    z_first, z_second = exchange(z_first, z_second, "gz")
    coarse, keep, inverse, ext = call(
        restrict,
        [
            ((GROUP, 4, 128), F32),
            ((12, 4, 4, 256), F32),
            ((3, 4, 4, 256), F32),
            ((PLANES - NU, 7, 8, 384), F32),
        ],
        [vmem] * 5,
        [
            pltpu.VMEM((NU, 7, 8, 384), F32),
            pltpu.VMEM((3, 6, 8, 384), F32),
            pltpu.VMEM((16, 8, 128), F32),
            pltpu.VMEM((64, 128), F32),
            pltpu.VMEM((8, 2, 8, 256), F32),
        ],
    )(wide, x_first, x_second, z_second, z_first)
    coarse = lax.all_to_all(coarse, ("gx", "gy"), 0, 0)
    (partial,) = call(
        multiply, [((8, 4, 128), F32)], [vmem] * 4, [pltpu.VMEM((128, 128), F32)]
    )(coarse, grad_parts, vec_parts, spread)
    partial = lax.all_to_all(partial, "gz", 0, 0)
    values = jnp.broadcast_to(jnp.sum(partial, 0)[None], (GROUP, 4, 128))
    values = lax.all_to_all(values, ("gx", "gy"), 0, 0)
    (out,) = call(
        finish,
        [((4, 3, 4, 4, 256), F32)],
        [vmem] * 6,
        [pltpu.VMEM((12, 16, 128), F32), pltpu.VMEM((16, 6, 8, 384), F32)],
    )(values, ext, keep, inverse, sign, select)
    return out


def solution(mesh):
    grid = P(None, "gx", "gy", "gz")
    return jax.shard_map(
        per_device,
        mesh=mesh,
        in_specs=(
            P(None, None, "gx", "gy", "gz"),
            grid,
            grid,
            grid,
            grid,
            grid,
            grid,
            P(("gx", "gy"), None),
            P(("gx", "gy"), None),
        ),
        out_specs=P(None, None, "gx", "gy", "gz"),
        check_vma=False,
    )
```

```python
import jax
import jax.numpy as jnp
from jax import lax
from jax.experimental import pallas as pl
from jax.experimental.pallas import tpu as pltpu
from jax.sharding import PartitionSpec as P

F32 = jnp.float32
BF16 = jnp.bfloat16
HIGHEST = lax.Precision.HIGHEST
NT = (((1,), (1,)), ((), ()))
NN = (((1,), (0,)), ((), ()))

B, NU, SG, GI, VI, CP = 0, 12, 15, 18, 22, 26
PLANES = 27
GROUP = 32


def faces(axis):
    hi = [(plane, 0) for plane in range(PLANES)]
    hi += [(NU + i, 1) for i in range(3) if i != axis]
    lo = [(plane, 0) for plane in range(PLANES) if plane >= NU or plane % 3 != axis]
    lo = [(plane, layer) for plane, layer in lo if plane != SG + axis]
    return hi, lo


def x_places(entries):
    places, at = {}, 0
    for entry in entries:
        if NU <= entry[0] < SG:
            places[entry] = (at, False)
            at += 1
    rest = [entry for entry in entries if entry not in places]
    for start in range(0, len(rest), 4):
        group = rest[start : start + 4]
        for j, entry in enumerate(group):
            places[entry] = (at, True) if j == 3 else (at + j, False)
        at += min(len(group), 3)
    return places, at


def put_slab(target, place, source):
    at, scattered = place
    if not scattered:
        target[at] = source[...]
        return
    for j in range(3):
        target[at + j, 0:1, :] = source[1 + 2 * j : 2 + 2 * j, :]
        target[at + j, 7:8, :] = source[2 + 2 * j : 3 + 2 * j, :]


def get_slab(source, place):
    at, scattered = place
    if not scattered:
        return source[at]
    blank = jnp.zeros((1, 256), F32)
    rows = [source[at + j, row : row + 1, :] for j in range(3) for row in (0, 7)]
    return jnp.concatenate([blank] + rows + [blank], 0)


def depth(axis):
    if axis == 0:
        return max(x_places(face)[1] for face in faces(0))
    return max(len(face) for face in faces(axis))


def col_lane(zb, k):
    return 252 + k if zb == 3 else 4 * zb + k


def call(body, outs, specs, scratch=(), limit=12, cost=None):
    return pl.pallas_call(
        body,
        out_shape=[jax.ShapeDtypeStruct(shape, dtype) for shape, dtype in outs],
        in_specs=[pl.BlockSpec(memory_space=space) for space in specs],
        out_specs=[pl.BlockSpec(memory_space=pltpu.VMEM)] * len(outs),
        scratch_shapes=list(scratch),
        cost_estimate=cost and pl.CostEstimate(flops=cost[0], bytes_accessed=cost[1], transcendentals=0),
        compiler_params=pltpu.CompilerParams(vmem_limit_bytes=limit * 1024 * 1024),
    )


def in_hbm(x):
    return pltpu.with_memory_space_constraint(x, pltpu.HBM)


def is_even(axis):
    return lax.rem(lax.axis_index(axis), 2) == 0


def send(even, hi, lo, first, second):
    @pl.when(even)
    def _():
        hi(first)
        lo(second)

    @pl.when(jnp.logical_not(even))
    def _():
        hi(second)
        lo(first)


def pack_y(rhs, sign, nu, sigma, gi, vi, cols, own, first, second, rhs_v, sign_v, cols_v, sems):
    copies = [
        pltpu.make_async_copy(rhs, rhs_v, sems.at[0]),
        pltpu.make_async_copy(sign, sign_v, sems.at[1]),
        pltpu.make_async_copy(cols, cols_v, sems.at[2]),
        pltpu.make_async_copy(nu, own.at[NU:SG], sems.at[3]),
        pltpu.make_async_copy(sigma, own.at[SG:GI], sems.at[4]),
        pltpu.make_async_copy(gi, own.at[GI:VI], sems.at[5]),
        pltpu.make_async_copy(vi, own.at[VI:CP], sems.at[6]),
    ]
    for copy in copies:
        copy.start()
    for copy in copies:
        copy.wait()
    lane = lax.broadcasted_iota(jnp.int32, (4, 256), 1)
    for x in range(4):
        plane = jnp.zeros((4, 256), F32)
        for k in range(4):
            for zb in range(4):
                plane = jnp.where(
                    lane == col_lane(zb, k), cols_v[k, x, :, zb : zb + 1].astype(F32), plane
                )
        own[CP, x] = plane
    for i in range(3):
        sign_of = sign_v[i].astype(F32)
        for p in range(4):
            own[3 * p + i] = rhs_v[p, i] * sign_of
    hi_list, lo_list = faces(1)

    def hi(target):
        for at, (plane, layer) in enumerate(hi_list):
            for x in range(4):
                target[at, x : x + 1, :] = own[plane, x, 3 - layer : 4 - layer, :]

    def lo(target):
        for at, (plane, layer) in enumerate(lo_list):
            for x in range(4):
                target[at, x : x + 1, :] = own[plane, x, layer : layer + 1, :]

    send(is_even("gy"), hi, lo, first, second)


def pack_x(own, y_second, y_first, wide, first, second):
    hi_list, lo_list = faces(1)
    hi_at = {entry: at for at, entry in enumerate(hi_list)}
    lo_at = {entry: at for at, entry in enumerate(lo_list)}

    def fill(minus, plus):
        zero = jnp.zeros((1, 256), F32)
        for plane in range(PLANES):
            for x in range(4):
                for row, where, source, key in (
                    (0, hi_at, minus, (plane, 1)),
                    (1, hi_at, minus, (plane, 0)),
                    (6, lo_at, plus, (plane, 0)),
                    (7, lo_at, plus, (plane, 1)),
                ):
                    value = source[where[key], x : x + 1, :] if key in where else zero
                    wide[plane, x, row : row + 1, :] = value
                wide[plane, x, 2:6, :] = own[plane, x]

    even_y = is_even("gy")

    @pl.when(even_y)
    def _():
        fill(y_second, y_first)

    @pl.when(jnp.logical_not(even_y))
    def _():
        fill(y_first, y_second)

    hi_x, lo_x = faces(0)

    def hi(target):
        for (plane, layer), place in x_places(hi_x)[0].items():
            put_slab(target, place, wide.at[plane, 3 - layer])

    def lo(target):
        for (plane, layer), place in x_places(lo_x)[0].items():
            put_slab(target, place, wide.at[plane, layer])

    send(is_even("gx"), hi, lo, first, second)


def slab_source(plane, x):
    hi_x, lo_x = faces(0)
    if 2 <= x < 6:
        return "own", x - 2
    side, entries, layer = ("minus", hi_x, 1 - x) if x < 2 else ("plus", lo_x, x - 6)
    places = x_places(entries)[0]
    key = (plane, layer)
    return (side, places[key]) if key in places else (None, None)


def pack_z(wide, x_first, x_second, after, first, second):
    lane = lax.broadcasted_iota(jnp.int32, (8, 128), 1)

    def fill(minus, plus, hi, lo):
        for x in range(7):
            low = jnp.zeros((8, 128), F32)
            high = jnp.zeros((8, 128), F32)
            for plane in range(PLANES):
                side, at = slab_source(plane, x)
                if side is None:
                    continue
                if side == "own":
                    source = wide[plane, at]
                else:
                    source = get_slab(minus if side == "minus" else plus, at)
                here = lane // 4 == plane
                low = jnp.where(here, pltpu.roll(source[:, 0:128], 4 * plane, 1), low)
                high = jnp.where(
                    here, pltpu.roll(source[:, 128:256], (4 * plane + 4) % 128, 1), high
                )
            lo[x] = low
            hi[x] = high

    even_x, even_z = is_even("gx"), is_even("gz")
    for x_even in (True, False):
        for z_even in (True, False):

            @pl.when((even_x == x_even) & (even_z == z_even))
            def _(x_even=x_even, z_even=z_even):
                minus, plus = (x_second, x_first) if x_even else (x_first, x_second)
                hi, lo = (first, second) if z_even else (second, first)
                fill(minus, plus, hi, lo)


def ahead(values, axis):
    return pltpu.roll(values, values.shape[axis] - 1, axis)


def behind(values, axis):
    return pltpu.roll(values, 1, axis)


def operate(v0, v1, v2, nu0, nu1, nu2, sg0, sg1, sg2):
    a0, a1, a2 = v0[:5], v1[:5], v2[:5]
    f0 = nu0 * ((ahead(a2, 1) - a2) - (ahead(a1, 2) - a1))
    f1 = nu1 * ((ahead(a0, 2) - a0) - (v2[1:6] - a2))
    f2 = nu2 * ((v1[1:6] - a1) - (ahead(a0, 1) - a0))
    r0 = (behind(f1, 2) - f1) - (behind(f2, 1) - f2) + sg0 * a0
    r1 = (f2[0:4] - f2[1:5]) - (behind(f0, 2)[1:5] - f0[1:5]) + sg1 * v1[1:5]
    r2 = (behind(f0, 1)[1:5] - f0[1:5]) - (f1[0:4] - f1[1:5]) + sg2 * v2[1:5]
    return r0, r1, r2


def restrict(
    wide, x_first, x_second, z_second, z_first, coarse, keep, inverse, ext, base, linv, sums, hot, own_weights
):
    lane = lax.broadcasted_iota(jnp.int32, (8, 128), 1)
    even_x, even_z = is_even("gx"), is_even("gz")

    def place(plane):
        return (base, plane) if plane < NU else (ext, plane - NU)

    def fill(minus, plus):
        zero = jnp.zeros((8, 256), F32)
        for plane in range(PLANES):
            target, to = place(plane)
            for x in (0, 1, 6):
                side, at = slab_source(plane, x)
                value = zero
                if side is not None:
                    value = get_slab(minus if side == "minus" else plus, at)
                target[to, x, :, 0:256] = value

    @pl.when(even_x)
    def _():
        fill(x_second, x_first)

    @pl.when(jnp.logical_not(even_x))
    def _():
        fill(x_first, x_second)

    base[:, 2:6, :, 0:256] = wide[0:NU]
    ext[:, 2:6, :, 0:256] = wide[NU:PLANES]
    for x in range(7):
        before = jnp.where(even_z, z_second[x], z_first[x])
        after = jnp.where(even_z, z_first[x], z_second[x])
        for plane in range(PLANES):
            target, to = place(plane)
            target[to, x, :, 256:384] = jnp.where(
                lane < 4,
                pltpu.roll(after, (128 - 4 * plane) % 128, 1),
                jnp.where(lane >= 124, pltpu.roll(before, (124 - 4 * plane) % 128, 1), 0.0),
            )
    nu0, nu1, nu2 = ext[0], ext[1], ext[2]
    n0, n1, n2 = nu0[1:7], nu1[1:7], nu2[1:7]
    floor = 0.1
    linv[0] = 1.0 / jnp.maximum(
        ext[3, 1:7] + 4.0 * ((n2 + behind(n2, 1)) + (n1 + behind(n1, 2))), floor
    )
    linv[1] = 1.0 / jnp.maximum(
        ext[4, 1:7] + 4.0 * ((n2 + nu2[0:6]) + (n0 + behind(n0, 2))), floor
    )
    linv[2] = 1.0 / jnp.maximum(
        ext[5, 1:7] + 4.0 * ((n1 + nu1[0:6]) + (n0 + behind(n0, 1))), floor
    )
    for i in range(3):
        inverse[i] = linv[i, 1:5, 2:6, 0:256]
    mine = (lax.axis_index("gx"), lax.axis_index("gy"), lax.axis_index("gz"))
    row = lax.broadcasted_iota(jnp.int32, (8, 256), 0)

    def pair(low, high):
        return jnp.where(row < 4, pltpu.roll(low, 6, 0), pltpu.roll(high, 2, 0))

    for k in range(8):
        for x in range(2):
            own_weights[k, x] = pair(
                ext[GI - NU + k, 2 * x + 2, :, 0:256], ext[GI - NU + k, 2 * x + 3, :, 0:256]
            )
    for x in range(2):
        plane = pair(ext[CP - NU, 2 * x + 2, :, 0:256], ext[CP - NU, 2 * x + 3, :, 0:256])
        for k in range(4):
            column = jnp.zeros((8, 128), F32)
            for zb in range(4):
                at = col_lane(zb, k)
                column = jnp.where(lane // 32 == zb, plane[:, at : at + 1], column)
            node = column.astype(jnp.int32)
            owner = node >> 2
            dx = (owner >> 5) - mine[0]
            dy = ((owner >> 3) & 3) - mine[1]
            dz = (owner & 7) - mine[2]
            side = jnp.where(dx == 1, 1, jnp.where(dx == -1, 2, 0))
            side = jnp.where(dy == 1, 3, jnp.where(dy == -1, 4, side))
            side = jnp.where(dz == 1, 5, jnp.where(dz == -1, 6, side))
            slot = 4 * side + (node & 3)
            at = 16 * k + 8 * x
            hot[at : at + 8] = jnp.where(slot == lane % 32, 1.0, 0.0)
    pick = (
        lax.broadcasted_iota(jnp.int32, (256, 128), 0) // 64
        == lax.broadcasted_iota(jnp.int32, (256, 128), 1) // 32
    )
    pick = jnp.where(pick, 1.0, 0.0).astype(BF16)

    def port(p):
        b0, b1, b2 = base[3 * p], base[3 * p + 1], base[3 * p + 2]
        u0, u1, u2 = b0[1:6] * linv[0, 0:5], b1[1:7] * linv[1], b2[1:7] * linv[2]
        r0, r1, r2 = operate(
            u0, u1, u2, ext[0, 1:6], ext[1, 1:6], ext[2, 1:6], ext[3, 1:6], ext[4, 2:6], ext[5, 2:6]
        )
        t0, t1, t2 = b0[1:6] - r0, b1[2:6] - r1, b2[2:6] - r2
        here = (t0[1:5], t1, t2)
        back = (t0[0:4], behind(t1, 1), behind(t2, 2))
        wide_u = (u0, u1, u2)
        parts = [((back[0] - here[0]) + (back[1] - here[1])) + (back[2] - here[2])]
        for i in range(3):
            kept = wide_u[i][1:5] + here[i] * linv[i, 1:5]
            keep[3 * p + i] = kept[:, 2:6, 0:256]
            parts.append(0.5 * (here[i] + back[i]))
        for kind in range(4):
            first = 0 if kind == 0 else 4
            part = parts[kind][:, :, 0:256]
            pairs = [pair(part[0], part[1]), pair(part[2], part[3])]
            products = [pairs[x] * own_weights[first + k, x] for k in range(4) for x in range(2)]
            product = jnp.concatenate(products, 0)
            top = product.astype(BF16)
            middle = (product - top.astype(F32)).astype(BF16)
            blocks = jnp.dot(top, pick, preferred_element_type=F32) + jnp.dot(
                middle, pick, preferred_element_type=F32
            )
            total = jnp.sum((blocks * hot[...]).reshape(8, 8, 128), axis=0)
            sums[4 * kind + p] = total

    for p in range(4):
        port(p)

    total = jnp.sum(sums[...], axis=1)
    total = total + pltpu.roll(total, 64, 1)
    total = total + pltpu.roll(total, 32, 1)
    quarter = lax.broadcasted_iota(jnp.int32, (4, 128), 1) // 32
    mixed = total[0:4]
    for kind in range(1, 4):
        mixed = jnp.where(quarter == kind, total[4 * kind : 4 * kind + 4], mixed)
    for g in range(GROUP):
        coarse[g] = mixed


def parts_of(value):
    top = value.astype(BF16)
    rest = value - top.astype(F32)
    middle = rest.astype(BF16)
    bottom = (rest - middle.astype(F32)).astype(BF16)
    return top, middle, bottom


def prepare(
    grad_hbm, vec_hbm, after, grad_parts, vec_parts, spread, select, grad_rows, vec_rows, sems
):
    copies = (
        pltpu.make_async_copy(grad_hbm, grad_rows, sems.at[0]),
        pltpu.make_async_copy(vec_hbm, vec_rows, sems.at[1]),
    )
    for copy in copies:
        copy.start()
    for copy in copies:
        copy.wait()
    for at, part in enumerate(parts_of(grad_rows[...])):
        grad_parts[at] = part
    for i in range(3):
        columns = pl.ds(1024 * i, 1024)
        for at, part in enumerate(parts_of(vec_rows[:, columns])):
            vec_parts[at, :, columns] = part
    z = lax.axis_index("gz")
    row = lax.broadcasted_iota(jnp.int32, (128, 128), 0)
    lane = lax.broadcasted_iota(jnp.int32, (128, 128), 1)
    gy = row >> 5
    side = (row & 31) >> 2
    gy_to = gy + jnp.where(side == 3, 1, 0) - jnp.where(side == 4, 1, 0)
    z_to = z + jnp.where(side == 5, 1, 0) - jnp.where(side == 6, 1, 0)
    hit = lane == 32 * gy_to + 4 * z_to + (row & 3)
    stay = hit & ((side == 0) | ((side >= 3) & (side <= 6)))
    for at, where in enumerate((stay, hit & (side == 1), hit & (side == 2))):
        spread[:, 128 * at : 128 * at + 128] = jnp.where(where, 1.0, 0.0).astype(BF16)
    row = lax.broadcasted_iota(jnp.int32, (96, 128), 0)
    lane = lax.broadcasted_iota(jnp.int32, (96, 128), 1)
    half = jnp.where((row >= 48) == (lane >= 64), 1.0, 0.0)
    for at in range(16):
        select[:, 128 * at : 128 * at + 128] = jnp.where((row & 15) == at, half, 0.0).astype(BF16)


def multiply(parts, grad_parts, vec_parts, spread, out, stacked):
    for gx in range(8):
        for gy in range(4):
            for kind in range(4):
                stacked[16 * gx + 4 * kind : 16 * gx + 4 * kind + 4, 32 * gy : 32 * gy + 32] = parts[
                    4 * gx + gy, :, 32 * kind : 32 * kind + 32
                ]
    moved = jnp.dot(
        jnp.concatenate(parts_of(stacked[...]), 0), spread[...], preferred_element_type=F32
    )
    moved = (moved[0:128] + moved[128:256]) + moved[256:384]
    tiles = []
    for gx in range(8):
        tile = moved[16 * gx : 16 * gx + 16, 0:128]
        if gx > 0:
            tile = tile + moved[16 * gx - 16 : 16 * gx, 128:256]
        if gx < 7:
            tile = tile + moved[16 * gx + 16 : 16 * gx + 32, 256:384]
        tiles.append(tile)
    vector = jnp.concatenate(tiles, 1)
    top, middle, bottom = (part.astype(F32) for part in parts_of(vector))

    def rows_of(kind):
        at = 4 * kind
        pieces = [part[at : at + 4] for part in (top, middle, bottom)]
        return jnp.concatenate(pieces + [jnp.zeros((4, 1024), F32)], 0).astype(BF16)

    def gathered(products):
        first, second, third = products
        small = third[0:4] + second[4:8] + first[8:12]
        return (small + (second[0:4] + first[4:8])) + first[0:4]

    def product(rows, weights):
        return lax.dot_general(rows, weights, NT, preferred_element_type=F32)

    rows = [rows_of(kind) for kind in range(4)]
    grad = gathered([product(rows[0], grad_parts[at]) for at in range(3)])
    vec = gathered(
        [
            sum(
                product(rows[1 + i], vec_parts[at, :, 1024 * i : 1024 * i + 1024])
                for i in range(3)
            )
            for at in range(3)
        ]
    )
    for z_at in range(8):
        out[z_at, :, 0:32] = grad
        out[z_at, :, 32:128] = vec


def finish(values, ext, keep, inverse, sign, select, out, dense, nodal):
    gx = lax.axis_index("gx")
    for tile in (0, 1, 10, 11):
        dense[tile] = jnp.zeros((16, 128), F32)
    for g in range(GROUP):
        at = 32 * (g % 4)
        dense[2 + g // 4, 0:4, at : at + 32] = values[g, :, 0:32]
        for c in range(3):
            q = 3 * g + c
            row = 4 + 4 * (q // 32)
            tile, at = 2 + (q % 32) // 4, 32 * (q % 4)
            dense[tile, row : row + 4, at : at + 32] = values[g, :, 32 + 32 * c : 64 + 32 * c]
    whole = jnp.concatenate([dense[gx + tile] for tile in range(5)], 1)
    split = jnp.concatenate(parts_of(whole), 0)
    blank = jnp.zeros((48, 640), BF16)
    sides = (jnp.concatenate([split, blank], 0), jnp.concatenate([blank, split], 0))
    node = lax.broadcasted_iota(jnp.int32, (8, 640), 1) + 128 * (gx - 2)
    lanes = (
        [col_lane(0, k) for k in range(4)],
        [col_lane(1, k) for k in range(4)],
        [col_lane(2, k) for k in range(4)],
        [col_lane(3, k) for k in range(4)],
        [256 + k for k in range(4)],
        [380 + k for k in range(4)],
    )
    for tile in range(3):
        taken = jnp.zeros((192, 96), F32)
        for half in range(2):
            rows = []
            for k in range(4):
                at = lanes[2 * tile + half][k]
                for x in range(1, 7):
                    column = ext[CP - NU, x, :, at : at + 1].astype(jnp.int32)
                    rows.append(jnp.where(column == node, 1.0, 0.0).astype(F32))
            hot = jnp.concatenate(rows, 0).astype(BF16)
            taken = taken + lax.dot_general(hot, sides[half], NT, preferred_element_type=F32)
        taken = taken.astype(BF16)
        for kind in range(4):
            first = GI - NU if kind == 0 else VI - NU
            spread = lax.dot_general(
                taken,
                select[:, 512 * kind : 512 * kind + 512],
                NN,
                preferred_element_type=F32,
            )
            for p in range(4):
                total = jnp.zeros((6, 8, 128), F32)
                for k in range(4):
                    total = total + ext[first + k, 1:7, :, 128 * tile : 128 * tile + 128] * spread[
                        48 * k : 48 * k + 48, 128 * p : 128 * p + 128
                    ].reshape(6, 8, 128)
                nodal[4 * kind + p, :, :, 128 * tile : 128 * tile + 128] = total

    shape = (6, 8, 384)
    x_at = lax.broadcasted_iota(jnp.int32, shape, 0)
    y_at = lax.broadcasted_iota(jnp.int32, shape, 1)
    z_at = lax.broadcasted_iota(jnp.int32, shape, 2)
    outside_x = (x_at == 0) & (lax.axis_index("gx") == 0)
    outside_y = (y_at == 1) & (lax.axis_index("gy") == 0)
    outside_z = (z_at == 383) & (lax.axis_index("gz") == 0)

    def port(p):
        g = nodal[p]
        v0, v1, v2 = nodal[4 + p], nodal[8 + p], nodal[12 + p]
        c0 = (g[1:6] - g[0:5]) + 0.5 * (v0[0:5] + v0[1:6])
        c1 = (ahead(g, 1) - g) + 0.5 * (v1 + ahead(v1, 1))
        c2 = (ahead(g, 2) - g) + 0.5 * (v2 + ahead(v2, 2))
        c0 = jnp.where(outside_x[0:5], 0.0, c0)
        c1 = jnp.where(outside_y, 0.0, c1)
        c2 = jnp.where(outside_z, 0.0, c2)
        r0, r1, r2 = operate(
            c0, c1, c2, ext[0, 1:6], ext[1, 1:6], ext[2, 1:6], ext[3, 1:6], ext[4, 2:6], ext[5, 2:6]
        )
        fields = ((c0[1:5], r0[1:5]), (c1[1:5], r1), (c2[1:5], r2))
        for i in range(3):
            c, r = fields[i]
            w = keep[3 * p + i] + (c[:, 2:6, 0:256] - r[:, 2:6, 0:256] * inverse[i])
            out[p, i] = sign[i].astype(F32) * w

    for p in range(4):
        port(p)


def exchange(first, second, axis):
    count = lax.axis_size(axis)

    def pairs(start):
        found = []
        for i in range(start, count - 1, 2):
            found += [(i, i + 1), (i + 1, i)]
        return found

    return lax.ppermute(first, axis, pairs(0)), lax.ppermute(second, axis, pairs(1))


def per_device(rhs, sign, nu, sigma, cols, gi, vi, grad_rows, vec_rows):
    vmem = pltpu.VMEM
    own, first, second = call(
        pack_y,
        [((PLANES, 4, 4, 256), F32)] + [((depth(1), 4, 256), F32)] * 2,
        [pl.ANY] * 7,
        [
            pltpu.VMEM((4, 3, 4, 4, 256), F32),
            pltpu.VMEM((3, 4, 4, 256), jnp.int32),
            pltpu.VMEM((4, 4, 4, 4), jnp.int32),
            pltpu.SemaphoreType.DMA((7,)),
        ],
    )(*[in_hbm(x) for x in (rhs, sign, nu, sigma, gi, vi, cols)])
    first, second = exchange(first, second, "gy")
    wide, x_first, x_second = call(
        pack_x,
        [((PLANES, 4, 8, 256), F32)] + [((depth(0), 8, 256), F32)] * 2,
        [vmem] * 3,
    )(own, second, first)
    grad_parts, vec_parts, spread, select = call(
        prepare,
        [((3, 32, 1024), BF16), ((3, 96, 3072), BF16), ((128, 384), BF16), ((96, 2048), BF16)],
        [pl.ANY] * 3,
        [
            pltpu.VMEM((32, 1024), F32),
            pltpu.VMEM((96, 3072), F32),
            pltpu.SemaphoreType.DMA((2,)),
        ],
        cost=(0, 8_000_000),
    )(in_hbm(grad_rows), in_hbm(vec_rows), x_first)
    x_first, x_second = exchange(x_first, x_second, "gx")
    z_first, z_second = call(pack_z, [((7, 8, 128), F32)] * 2, [vmem] * 3 + [pl.ANY])(
        wide, x_first, x_second, select
    )
    z_first, z_second = exchange(z_first, z_second, "gz")
    coarse, keep, inverse, ext = call(
        restrict,
        [
            ((GROUP, 4, 128), F32),
            ((12, 4, 4, 256), F32),
            ((3, 4, 4, 256), F32),
            ((PLANES - NU, 7, 8, 384), F32),
        ],
        [vmem] * 5,
        [
            pltpu.VMEM((NU, 7, 8, 384), F32),
            pltpu.VMEM((3, 6, 8, 384), F32),
            pltpu.VMEM((16, 8, 128), F32),
            pltpu.VMEM((64, 128), F32),
            pltpu.VMEM((8, 2, 8, 256), F32),
        ],
    )(wide, x_first, x_second, z_second, z_first)
    coarse = lax.all_to_all(coarse, ("gx", "gy"), 0, 0)
    (partial,) = call(
        multiply, [((8, 4, 128), F32)], [vmem] * 4, [pltpu.VMEM((128, 128), F32)]
    )(coarse, grad_parts, vec_parts, spread)
    partial = lax.all_to_all(partial, "gz", 0, 0)
    values = jnp.broadcast_to(jnp.sum(partial, 0)[None], (GROUP, 4, 128))
    values = lax.all_to_all(values, ("gx", "gy"), 0, 0)
    (out,) = call(
        finish,
        [((4, 3, 4, 4, 256), F32)],
        [vmem] * 6,
        [pltpu.VMEM((12, 16, 128), F32), pltpu.VMEM((16, 6, 8, 384), F32)],
    )(values, ext, keep, inverse, sign, select)
    return out


def solution(mesh):
    grid = P(None, "gx", "gy", "gz")
    return jax.shard_map(
        per_device,
        mesh=mesh,
        in_specs=(
            P(None, None, "gx", "gy", "gz"),
            grid,
            grid,
            grid,
            grid,
            grid,
            grid,
            P(("gx", "gy"), None),
            P(("gx", "gy"), None),
        ),
        out_specs=P(None, None, "gx", "gy", "gz"),
        check_vma=False,
    )
```
